256 devices in a mesh: tok: 4 (over z_lo), hid: 64 (over y, z_hi, x, core).
Axes of the slice: x: 4, y: 4, z: 8 (z_hi: 2, z_lo: 4; z = z_hi * 4 + z_lo), core: 2. Of those that a mesh axis runs over, the one named last changes fastest.
Arguments:
- tokens: bfloat16 [512, 8192], P('hid', 'tok'), may hold values from -20 to 20
- gate_weight: bfloat16 [8192, 26624], P('tok', 'hid'), may hold values from -0.0625 to 0.0625
- up_weight: bfloat16 [8192, 26624], P('tok', 'hid'), may hold values from -0.0625 to 0.0625
- down_weight: bfloat16 [26624, 8192], P('hid', 'tok'), may hold values from -0.0390625 to 0.0390625
- out_grad: bfloat16 [512, 8192], P('hid', 'tok'), may hold values from -6 to 6
- amax_prior: float32 [4], replicated, may hold values from 4 to 60
Outputs:
- output: bfloat16 [512, 8192], P('hid', 'tok')
- input_grad: bfloat16 [512, 8192], P('hid', 'tok')
- gate_grad: bfloat16 [8192, 26624], P('tok', 'hid')
- up_grad: bfloat16 [8192, 26624], P('tok', 'hid')
- down_grad: bfloat16 [26624, 8192], P('hid', 'tok')
- amaxes: float32 [6], replicated
The draws below stay inside these ranges and needn't reach their ends.
All inputs are finite; a program needn't handle non-finite values. Where the reference program divides by a largest or mean magnitude, that divisor is 1e-20 or more.
Results may differ from the reference program's by a relative error of at most 0.0081.
Values may be sent and summed in bfloat16 or wider, within the bound.
A program may use at most 128 MiB of HBM per device.

```python
import math
import jax
import jax.numpy as jnp
from jax import lax

D = 8192
FF = 26624
TOKENS = 512


def draw_tokens(key, part):
    key = jax.random.fold_in(key, 11)
    key_rows, key_base = jax.random.split(key, 2)
    rows = jnp.exp(jax.random.uniform(key_rows, (TOKENS, 1), jnp.float32, math.log(0.5), math.log(5.0)))
    base = jnp.clip(jax.random.normal(key_base, (TOKENS, D), jnp.float32), -4.0, 4.0)
    return (base * rows).astype(jnp.bfloat16)


def draw_amax_prior(key, part):
    key = jax.random.fold_in(key, 23)
    lows = jnp.array([6.0, 20.0, 4.0, 4.0], jnp.float32)
    highs = jnp.array([12.0, 60.0, 5.0, 10.0], jnp.float32)
    unit = jax.random.uniform(key, (4,), jnp.float32)
    return lows + (highs - lows) * unit


def block_levels(rng, shape, cuts, least, high):
    gain, own = 1.0, jax.random.fold_in(rng, 6)
    for dim, parts in cuts:
        steps = jnp.exp(jax.random.uniform(jax.random.fold_in(own, dim), (parts,), jnp.float32, least / len(cuts), high / len(cuts)))
        gain = gain * jnp.repeat(steps, shape[dim] // parts).reshape([-1 if axis == dim else 1 for axis in range(len(shape))])
    return gain


def normal_values(stream_key, extent, spread, limit, cuts=(), dtype=jnp.bfloat16):
    values = spread * jax.random.normal(stream_key, extent, jnp.float32)
    if cuts:
        values = values * block_levels(stream_key, extent, cuts, -0.22, 0.18)
    return jnp.clip(values, -limit, limit).astype(dtype)


def setup_inputs(seed: int = 0) -> dict:
    streams_of = jax.random.split(jax.random.key(seed), 7)
    tokens = draw_tokens(jax.random.fold_in(streams_of[6], 71), 0)
    gate_weight = normal_values(streams_of[1], (D, FF), D ** -0.5, 0.0625, ((0, 4), (1, 64)))
    up_weight = normal_values(streams_of[2], (D, FF), D ** -0.5, 0.0625, ((0, 4), (1, 64)))
    down_weight = normal_values(streams_of[3], (FF, D), FF ** -0.5, 0.0390625, ((0, 64), (1, 4)))
    out_grad = normal_values(streams_of[4], (TOKENS, D), 1.0, 6.0, ((0, 64), (1, 4)))
    amax_prior = draw_amax_prior(jax.random.fold_in(streams_of[6], 71), 0)
    return {"tokens": tokens, "gate_weight": gate_weight, "up_weight": up_weight, "down_weight": down_weight, "out_grad": out_grad, "amax_prior": amax_prior}


def quantize(value, scale):
    return jnp.clip(value / scale, -448.0, 448.0).astype(jnp.bfloat16)


def contract_last(left, right):
    return lax.dot_general(left, right, (((1,), (1,)), ((), ())), preferred_element_type=jnp.float32)


def contract_first(left, right):
    return lax.dot_general(left, right, (((0,), (0,)), ((), ())), preferred_element_type=jnp.float32)


def reference(tokens, gate_weight, up_weight, down_weight, out_grad, amax_prior):
    scales = amax_prior / 448.0
    xq = quantize(tokens.astype(jnp.float32), scales[0])
    gate = jnp.dot(xq, gate_weight, preferred_element_type=jnp.float32) * scales[0]
    up = jnp.dot(xq, up_weight, preferred_element_type=jnp.float32) * scales[0]
    sig = jax.nn.sigmoid(gate)
    act = gate * sig
    hidden = act * up
    hq = quantize(hidden, scales[1])
    output = (jnp.dot(hq, down_weight, preferred_element_type=jnp.float32) * scales[1]).astype(jnp.bfloat16)
    grad_q = quantize(out_grad.astype(jnp.float32), scales[2])
    dhidden = contract_last(grad_q, down_weight) * scales[2]
    dgate = dhidden * up * sig * (1.0 + gate * (1.0 - sig))
    dup = dhidden * act
    dgq = quantize(dgate, scales[3])
    duq = quantize(dup, scales[3])
    input_grad = ((contract_last(dgq, gate_weight) + contract_last(duq, up_weight)) * scales[3]).astype(jnp.bfloat16)
    wgate = contract_first(xq, dgq) * (scales[0] * scales[3])
    wup = contract_first(xq, duq) * (scales[0] * scales[3])
    wdown = contract_first(hq, grad_q) * (scales[1] * scales[2])
    amax_gu = jnp.maximum(jnp.max(jnp.abs(wgate)), jnp.max(jnp.abs(wup)))
    amax_down = jnp.max(jnp.abs(wdown))
    peaks = jnp.stack([
        jnp.max(jnp.abs(tokens.astype(jnp.float32))),
        jnp.max(jnp.abs(hidden)),
        jnp.max(jnp.abs(out_grad.astype(jnp.float32))),
        jnp.maximum(jnp.max(jnp.abs(dgate)), jnp.max(jnp.abs(dup))),
        amax_gu,
        amax_down,
    ])
    gate_grad = (wgate / (amax_gu + 1e-6)).astype(jnp.bfloat16)
    up_grad = (wup / (amax_gu + 1e-6)).astype(jnp.bfloat16)
    down_grad = (wdown / (amax_down + 1e-6)).astype(jnp.bfloat16)
    amaxes = jnp.log(peaks + 1e-6)
    return output, input_grad, gate_grad, up_grad, down_grad, amaxes
```

```python
import jax
import jax.numpy as jnp
from jax import lax
from jax.experimental import pallas as pl
from jax.experimental.pallas import tpu as pltpu
from jax.sharding import PartitionSpec as P

MESH = pl.DeviceIdType.MESH
BF = jnp.bfloat16
F32 = jnp.float32
HALF = 1024
WIDE = 896
FILL = 512


def contract_last(left, right):
    return lax.dot_general(left, right, (((1,), (1,)), ((), ())), preferred_element_type=F32)


def contract_first(left, right):
    return lax.dot_general(left, right, (((0,), (0,)), ((), ())), preferred_element_type=F32)


def quantize(value, scale):
    return jnp.clip(value / scale, -448.0, 448.0).astype(BF)


class Links:
    def __init__(self, send, recv):
        self.send, self.recv, self.used, self.open = send, recv, 0, []

    def slots(self, count):
        first = self.used
        self.used += count
        return first

    def copy(self, src, dst, slot, device):
        return pltpu.make_async_remote_copy(
            src_ref=src,
            dst_ref=dst,
            send_sem=self.send.at[slot],
            recv_sem=self.recv.at[slot],
            device_id=device,
            device_id_type=MESH,
        )

    def start(self, src, dst, slot, device):
        copy = self.copy(src, dst, slot, device)
        copy.start()
        self.open.append(copy)

    def arrived(self, dst, slot, device):
        self.copy(dst, dst, slot, device).wait_recv()

    def finish(self):
        for copy in self.open:
            copy.wait_send()


N_SEMS = 160


def kernel(
    prior, tokens, out_grad, weights_hbm, down_hbm,
    out_ref, in_grad_ref, wide_hbm, wdown_hbm, peaks_ref,
    xb, gb, wide_w, down_w, swap_out, swap_in,
    part, keep, got1, send2, got2,
    dpart, dkeep, dgot1, dsend2, dgot2,
    hb, db,
    o_part, o_core, o_ring, o_send, o_got, o_zs, o_zr, o_fin, o_fr,
    i_part, i_core, i_ring, i_ring2, i_send, i_send2, i_got, i_got2, i_zs, i_zr, i_fin, i_fr,
    wide_g, down_g, max_s, max_r,
    send_sem, recv_sem, load_sem, store_sem,
):
    t = lax.axis_index("tok")
    h = lax.axis_index("hid")
    y, zh, x, c = h // 16, (h // 8) % 2, (h // 2) % 4, h % 2
    p, s = t % 2, t // 2

    def device(dt=0, dy=0, dz=0, dx=0, dc=0):
        hid = ((((y + dy) % 4) * 2 + (zh + dz) % 2) * 4 + (x + dx) % 4) * 2 + (c + dc) % 2
        return ((t + dt) % 4, hid)

    def beside():
        return (t + 1 - 2 * p, h)

    peers = [device(dx=d, dc=e) for d in range(4) for e in range(2) if d or e]
    peers += [device(dy=d) for d in (1, 2, 3)]
    peers += [device(dt=d, dz=e) for d in range(4) for e in range(2) if d or e]
    barrier = pltpu.get_barrier_semaphore()
    for peer in peers:
        pl.semaphore_signal(barrier, inc=1, device_id=peer, device_id_type=MESH)

    load_w = pltpu.make_async_copy(weights_hbm, wide_w, load_sem.at[0])
    load_w.start()
    load_d = pltpu.make_async_copy(down_hbm, down_w.at[pl.ds(0, 416)], load_sem.at[1])
    load_d.start()
    down_w[pl.ds(416, 96), :] = jnp.zeros((96, 2048), BF)

    s0, s1, s2, s3 = [prior[i] / 448.0 for i in range(4)]
    mine = pl.ds(pl.multiple_of(c * HALF, HALF), HALF)
    other = pl.ds(pl.multiple_of((1 - c) * HALF, HALF), HALF)

    tok_f = tokens[...].astype(F32)
    og_f = out_grad[...].astype(F32)
    max_x = jnp.max(jnp.abs(tok_f))
    max_g = jnp.max(jnp.abs(og_f))
    swap_out[pl.ds(0, 8), :] = quantize(tok_f, s0).astype(F32)
    swap_out[pl.ds(8, 8), :] = quantize(og_f, s2).astype(F32)

    links = Links(send_sem, recv_sem)
    core = device(dc=1)

    pl.semaphore_wait(barrier, len(peers))

    slot = links.slots(1)
    links.start(swap_out.at[:, other], swap_in, slot, core)
    links.arrived(swap_in, slot, core)
    own = swap_out[:, mine]
    theirs = swap_in[...]
    low = jnp.where(c == 0, own, theirs)
    high = jnp.where(c == 0, theirs, own)
    xb[y, zh, x, :, mine] = jnp.concatenate([low[0:8], high[0:8]], axis=0).astype(BF)
    gb[y, zh, x, :, mine] = jnp.concatenate([low[8:16], high[8:16]], axis=0).astype(BF)

    def step_x(d):
        return device(dx=d)

    def step_y(d):
        return device(dy=d)

    tx1, tx2, tz = links.slots(4), links.slots(4), links.slots(1)
    ty1, ty2, tc = links.slots(4), links.slots(4), links.slots(4)
    gy1, gy2, gz = links.slots(4), links.slots(4), links.slots(1)
    gx1, gx2, gc = links.slots(4), links.slots(4), links.slots(4)
    away = device(dz=1)
    xblock = xb.at[y, zh, x, :, mine]
    gblock = gb.at[y, zh, x, :, mine]
    links.start(xblock, xblock, tz, away)
    for d in (1, 3, 2):
        links.start(xblock, xblock, tx1 + d, step_x(d))
    links.start(gblock, gblock, gz, away)
    for d in (1, 3, 2):
        links.start(gblock, gblock, gy1 + d, step_y(d))
    xblock2 = xb.at[y, 1 - zh, x, :, mine]
    gblock2 = gb.at[y, 1 - zh, x, :, mine]
    links.arrived(xblock2, tz, away)
    for d in (1, 3, 2):
        links.start(xblock2, xblock2, tx2 + d, step_x(d))
    links.arrived(gblock2, gz, away)
    for d in (1, 3, 2):
        links.start(gblock2, gblock2, gy2 + d, step_y(d))
    for z, tx, ty, gy, gx in ((zh, tx1, ty1, gy1, gx1), (1 - zh, tx2, ty2, gy2, gx2)):
        for d in (1, 3, 2):
            links.arrived(xb.at[y, z, (x - d) % 4, :, mine], tx + d, step_x(4 - d))
        rows = xb.at[y, z, :, :, mine]
        for d in (1, 3, 2):
            links.start(rows, rows, ty + d, step_y(d))
        for d in (1, 3, 2):
            links.arrived(gb.at[(y - d) % 4, z, x, :, mine], gy + d, step_y(4 - d))
        rows = gb.at[:, z, x, :, mine]
        for d in (1, 3, 2):
            links.start(rows, rows, gx + d, step_x(d))
    rows = xb.at[y, :, :, :, mine]
    links.start(rows, rows, tc, core)
    rows = gb.at[:, :, x, :, mine]
    links.start(rows, rows, gc, core)

    load_w.wait()
    load_d.wait()

    order = ((1 - p) + 2 * (1 - s), (1 - p) + 2 * s, p + 2 * (1 - s), p + 2 * s)
    r1, r2 = links.slots(2), links.slots(1)
    d1, d2 = links.slots(2), links.slots(1)
    partner = beside()
    far = device(dt=2)
    gdone = (1, 3, 2, None)
    for j, k in enumerate(order):
        yk = (y + k) % 4
        rows = xb.at[yk, :, :, :, mine]

        @pl.when(k != 0)
        def _():
            for z, ty in ((zh, ty1), (1 - zh, ty2)):
                links.arrived(xb.at[yk, z, :, :, mine], ty + (4 - k), device(dy=k))
            links.copy(rows, rows, tc + k, core).start()

        g = gdone[j]
        if g is not None:
            for z, gx in ((zh, gx1), (1 - zh, gx2)):
                links.arrived(gb.at[:, z, (x + g) % 4, :, mine], gx + (4 - g), step_x(g))
            rows_g = gb.at[:, :, (x + g) % 4, :, mine]
            links.start(rows_g, rows_g, gc + g, core)
        links.arrived(xb.at[yk, :, :, :, other], tc + k, core)
        value = jnp.dot(
            xb[yk].reshape(128, 2048), wide_w[...], preferred_element_type=F32
        )
        if j < 2:
            part[j] = value.astype(BF)
            to = 1 - s if j == 0 else s
            links.start(part.at[j], got1.at[to], r1 + to, partner)
        else:
            keep[j - 2] = value
    for g in (0, 1, 3, 2):
        links.arrived(gb.at[:, :, (x + g) % 4, :, other], gc + g, core)
    for j, k in enumerate(order):
        yk = (y + k) % 4
        value = contract_last(gb[yk].reshape(128, 2048), down_w[...])
        if j < 2:
            dpart[j] = value.astype(BF)
            to = 1 - s if j == 0 else s
            links.start(dpart.at[j], dgot1.at[to], d1 + to, partner)
        else:
            dkeep[j - 2] = value
    links.arrived(got1.at[1 - s], r1 + (1 - s), partner)
    send2[...] = (keep[0] + got1[1 - s].astype(F32)).astype(BF)
    links.start(send2, got2, r2, far)
    links.arrived(dgot1.at[1 - s], d1 + (1 - s), partner)
    dsend2[...] = (dkeep[0] + dgot1[1 - s].astype(F32)).astype(BF)
    links.start(dsend2, dgot2, d2, far)

    lane = lax.broadcasted_iota(jnp.int32, (128, FILL), 1)
    inside = lane < 416
    yt = (y + t) % 4
    h1, h2, h3 = links.slots(1), links.slots(1), links.slots(1)
    g1, g2, g3 = links.slots(1), links.slots(1), links.slots(1)

    links.arrived(got1.at[s], r1 + s, partner)
    links.arrived(got2, r2, far)
    both = (keep[1] + got1[s].astype(F32) + got2[...].astype(F32)) * s0
    gate = jnp.where(inside, both[:, :FILL], 0.0)
    up = jnp.where(inside, pltpu.roll(both, WIDE - 416, 1)[:, :FILL], 0.0)
    sig = jax.nn.sigmoid(gate)
    act = gate * sig
    hidden = act * up
    max_h = jnp.max(jnp.abs(hidden))
    hb[yt] = quantize(hidden, s1)
    links.start(hb.at[yt], hb.at[yt], h1, far)
    links.start(hb.at[yt], hb.at[yt], h2, partner)

    links.arrived(dgot1.at[s], d1 + s, partner)
    links.arrived(dgot2, d2, far)
    dhidden = (dkeep[1] + dgot1[s].astype(F32) + dgot2[...].astype(F32)) * s2
    dgate = dhidden * up * sig * (1.0 + gate * (1.0 - sig))
    dup = dhidden * act
    max_p = jnp.maximum(jnp.max(jnp.abs(dgate)), jnp.max(jnp.abs(dup)))
    room = jnp.zeros((128, WIDE - FILL), F32)
    dgq = jnp.concatenate([quantize(dgate, s3).astype(F32), room], axis=1)
    duq = jnp.concatenate([quantize(dup, s3).astype(F32), room], axis=1)
    db[yt] = (dgq + pltpu.roll(duq, 416, 1)).astype(BF)
    links.start(db.at[yt], db.at[yt], g1, far)
    links.start(db.at[yt], db.at[yt], g2, partner)

    yf = (y + (t + 2) % 4) % 4
    yp = (y + partner[0]) % 4
    ypf = (y + (partner[0] + 2) % 4) % 4
    links.arrived(hb.at[yf], h1, far)
    links.start(hb.at[yf], hb.at[yf], h3, partner)

    o_cs, i_cs = links.slots(4), links.slots(4)

    def out_block(at, n):
        value = jnp.dot(hb[at], down_w[...], preferred_element_type=F32)
        o_part[at] = value.astype(BF).reshape(2, 4, 16, 2048)
        links.start(o_part.at[at, :, :, :, other], o_core.at[at], o_cs + n, core)

    def in_block(at, n):
        value = contract_last(db[at], wide_w[...])
        i_part[at] = value.astype(BF).reshape(2, 4, 16, 2048)
        links.start(i_part.at[at, :, :, :, other], i_core.at[at], i_cs + n, core)

    blocks = (yt, yf, yp, ypf)

    out_block(yt, 0)
    out_block(yf, 1)
    links.arrived(db.at[yf], g1, far)
    links.start(db.at[yf], db.at[yf], g3, partner)
    links.arrived(hb.at[yp], h2, partner)
    links.arrived(hb.at[ypf], h3, partner)
    out_block(yp, 2)
    out_block(ypf, 3)

    o_y, o_x, o_z, o_c = links.slots(4), links.slots(4), links.slots(1), links.slots(1)
    for n, at in enumerate(blocks):
        links.arrived(o_core.at[at], o_cs + n, core)
        value = o_part[at, :, :, :, mine].astype(F32) + o_core[at].astype(F32)
        o_core[at] = value.astype(BF)
    for d in (1, 3, 2):
        links.start(o_core.at[(y + d) % 4], o_ring.at[d - 1], o_y + d, step_y(d))

    flipped = hb[...].reshape(512, FILL).astype(F32).T.astype(BF)

    def down_tile(i, top):
        columns = pl.ds(pl.multiple_of(i * 256, 256), 256)
        rows = gb[:, :, :, :, columns].reshape(512, 256)
        value = jnp.dot(flipped, rows, preferred_element_type=F32)[:416] * (s1 * s2)
        down_g[:, columns] = value.astype(BF)
        return jnp.maximum(top, jnp.max(jnp.abs(value)))

    max_d = lax.fori_loop(0, 8, down_tile, jnp.float32(0.0))
    store_d = pltpu.make_async_copy(down_g, wdown_hbm, store_sem.at[0])
    store_d.start()

    in_block(yt, 0)
    in_block(yf, 1)

    for d in (1, 3, 2):
        links.arrived(o_ring.at[d - 1], o_y + d, step_y(4 - d))
    total = o_core[y].astype(F32)
    for d in (1, 2, 3):
        total = total + o_ring[d - 1].astype(F32)
    o_send[...] = total.astype(BF)
    for d in (1, 3, 2):
        links.start(o_send.at[:, (x + d) % 4], o_got.at[d - 1], o_x + d, step_x(d))

    links.arrived(db.at[yp], g2, partner)
    links.arrived(db.at[ypf], g3, partner)
    in_block(yp, 2)
    in_block(ypf, 3)

    def rest(links, send, got, x_slot, z_slot, zs, zr, device_of, index):
        for d in (1, 3, 2):
            links.arrived(got.at[d - 1], x_slot + d, device_of(4 - d))
        total = send[:, index].astype(F32) if len(send.shape) == 4 else None
        for d in (1, 2, 3):
            total = total + got[d - 1].astype(F32)
        zs[...] = total
        links.start(zs.at[1 - zh], zr, z_slot, away)

    rest(links, o_send, o_got, o_x, o_z, o_zs, o_zr, step_x, x)

    i_y, i_x, i_z, i_c = links.slots(4), links.slots(4), links.slots(1), links.slots(1)
    j_y, j_x, j_z = links.slots(4), links.slots(4), links.slots(1)
    for n, at in enumerate(blocks):
        links.arrived(i_core.at[at], i_cs + n, core)
        value = i_part[at, :, :, :, mine].astype(F32) + i_core[at].astype(F32)
        i_core[at] = value.astype(BF)
    left, right = pl.ds(0, 512), pl.ds(512, 512)
    for d in (1, 3, 2):
        links.start(
            i_core.at[(y + d) % 4, :, :, :, left], i_ring.at[d - 1], i_y + d, step_y(d)
        )
        links.start(
            i_core.at[:, :, (x + d) % 4, :, right], i_ring2.at[d - 1], j_x + d, step_x(d)
        )

    links.arrived(o_zr, o_z, away)
    o_fin[...] = o_zs[zh] + o_zr[...]
    rows_other = pl.ds(pl.multiple_of((1 - c) * 8, 8), 8)
    rows_mine = pl.ds(pl.multiple_of(c * 8, 8), 8)
    links.start(o_fin.at[rows_other], o_fr, o_c, core)

    def wide_tile(i, top):
        columns = pl.ds(pl.multiple_of(i * 256, 256), 256)
        rows = xb[:, :, :, :, columns].reshape(512, 256)
        value = contract_first(rows, db[...].reshape(512, WIDE)) * (s0 * s3)
        wide_g[columns, :] = value.astype(BF)
        return jnp.maximum(top, jnp.max(jnp.abs(value)))

    max_w = lax.fori_loop(0, 8, wide_tile, jnp.float32(0.0))
    store_w = pltpu.make_async_copy(wide_g, wide_hbm, store_sem.at[1])
    store_w.start()

    row = lax.broadcasted_iota(jnp.int32, (8, 128), 0)
    tops = jnp.zeros((8, 128), F32)
    for n, value in enumerate((max_x, max_h, max_g, max_p, max_w, max_d)):
        tops = jnp.where(row == n, value, tops)

    def send_tops(stage, value, offsets):
        first = links.slots(len(offsets))
        max_s[stage] = value
        for n, offset in enumerate(offsets):
            links.start(max_s.at[stage], max_r.at[stage, n], first + n, device(**offset))
        return first

    def take_tops(stage, value, offsets, first):
        for n, offset in enumerate(offsets):
            back = {name: -d for name, d in offset.items()}
            links.arrived(max_r.at[stage, n], first + n, device(**back))
            value = jnp.maximum(value, max_r[stage, n])
        return value

    plane = [dict(dx=d, dc=e) for d in range(4) for e in range(2) if d or e]
    depth = [dict(dt=d, dz=e) for d in range(4) for e in range(2) if d or e]
    column = [dict(dy=d) for d in (1, 2, 3)]
    first = send_tops(0, tops, plane)

    for d in (1, 3, 2):
        links.arrived(i_ring.at[d - 1], i_y + d, step_y(4 - d))
    total = i_core[y, :, :, :, left].astype(F32)
    for d in (1, 2, 3):
        total = total + i_ring[d - 1].astype(F32)
    i_send[...] = total.astype(BF)
    for d in (1, 3, 2):
        links.start(i_send.at[:, (x + d) % 4], i_got.at[d - 1], i_x + d, step_x(d))
    for d in (1, 3, 2):
        links.arrived(i_ring2.at[d - 1], j_x + d, step_x(4 - d))
    total = i_core[:, :, x, :, right].astype(F32)
    for d in (1, 2, 3):
        total = total + i_ring2[d - 1].astype(F32)
    i_send2[...] = total.astype(BF)
    for d in (1, 3, 2):
        links.start(i_send2.at[(y + d) % 4], i_got2.at[d - 1], j_y + d, step_y(d))

    tops = take_tops(0, tops, plane, first)
    first = send_tops(1, tops, column)

    for d in (1, 3, 2):
        links.arrived(i_got.at[d - 1], i_x + d, step_x(4 - d))
    total = i_send[:, x].astype(F32)
    for d in (1, 2, 3):
        total = total + i_got[d - 1].astype(F32)
    i_zs[:, :, left] = total
    for d in (1, 3, 2):
        links.arrived(i_got2.at[d - 1], j_y + d, step_y(4 - d))
    total = i_send2[y].astype(F32)
    for d in (1, 2, 3):
        total = total + i_got2[d - 1].astype(F32)
    i_zs[:, :, right] = total
    links.start(i_zs.at[1 - zh], i_zr, i_z, away)

    tops = take_tops(1, tops, column, first)
    first = send_tops(2, tops, depth)

    links.arrived(o_fr, o_c, core)
    out_ref[:, mine] = (o_fin[rows_mine, :] * s1).astype(BF)
    out_ref[:, other] = (o_fr[...] * s1).astype(BF)

    links.arrived(i_zr, i_z, away)
    i_fin[...] = i_zs[zh] + i_zr[...]
    links.start(i_fin.at[rows_other], i_fr, i_c, core)

    tops = take_tops(2, tops, depth, first)
    peaks_ref[pl.ds(0, 8), :] = tops
    peaks_ref[pl.ds(8, 8), :] = jnp.log(tops + 1e-6)

    links.arrived(i_fr, i_c, core)
    in_grad_ref[:, mine] = (i_fin[rows_mine, :] * s3).astype(BF)
    in_grad_ref[:, other] = (i_fr[...] * s3).astype(BF)

    for k in (1, 2, 3):
        rows = xb.at[0, :, :, :, mine]
        links.copy(rows, rows, tc + k, core).wait_send()
    links.finish()
    store_d.wait()
    store_w.wait()
    assert links.used <= N_SEMS


def shards(tokens, gate_weight, up_weight, down_weight, out_grad, amax_prior):
    width = gate_weight.shape[1]
    weights = jnp.concatenate(
        [gate_weight, up_weight, jnp.zeros((2048, WIDE - 2 * width), BF)], axis=1
    )
    vmem = pl.BlockSpec(memory_space=pltpu.VMEM)
    hbm = pl.BlockSpec(memory_space=pl.ANY)
    V = pltpu.VMEM
    output, input_grad, wide, wdown, peaks = pl.pallas_call(
        kernel,
        out_shape=(
            jax.ShapeDtypeStruct((8, 2048), BF),
            jax.ShapeDtypeStruct((8, 2048), BF),
            jax.ShapeDtypeStruct((2048, WIDE), BF),
            jax.ShapeDtypeStruct((416, 2048), BF),
            jax.ShapeDtypeStruct((16, 128), F32),
        ),
        in_specs=[pl.BlockSpec(memory_space=pltpu.SMEM), vmem, vmem, hbm, hbm],
        out_specs=(vmem, vmem, hbm, hbm, vmem),
        scratch_shapes=[
            V((4, 2, 4, 16, 2048), BF), V((4, 2, 4, 16, 2048), BF),
            V((2048, WIDE), BF), V((FILL, 2048), BF),
            V((16, 2048), F32), V((16, HALF), F32),
            V((2, 128, WIDE), BF), V((2, 128, WIDE), F32), V((2, 128, WIDE), BF),
            V((128, WIDE), BF), V((128, WIDE), BF),
            V((2, 128, FILL), BF), V((2, 128, FILL), F32), V((2, 128, FILL), BF),
            V((128, FILL), BF), V((128, FILL), BF),
            V((4, 128, FILL), BF), V((4, 128, WIDE), BF),
            V((4, 2, 4, 16, 2048), BF), V((4, 2, 4, 16, HALF), BF), V((3, 2, 4, 16, HALF), BF),
            V((2, 4, 16, HALF), BF), V((3, 2, 16, HALF), BF),
            V((2, 16, HALF), F32), V((16, HALF), F32), V((16, HALF), F32), V((8, HALF), F32),
            V((4, 2, 4, 16, 2048), BF), V((4, 2, 4, 16, HALF), BF),
            V((3, 2, 4, 16, 512), BF), V((3, 4, 2, 16, 512), BF),
            V((2, 4, 16, 512), BF), V((4, 2, 16, 512), BF),
            V((3, 2, 16, 512), BF), V((3, 2, 16, 512), BF),
            V((2, 16, HALF), F32), V((16, HALF), F32), V((16, HALF), F32), V((8, HALF), F32),
            V((2048, WIDE), BF), V((416, 2048), BF),
            V((3, 8, 128), F32), V((3, 7, 8, 128), F32),
            pltpu.SemaphoreType.DMA((N_SEMS,)), pltpu.SemaphoreType.DMA((N_SEMS,)),
            pltpu.SemaphoreType.DMA((2,)), pltpu.SemaphoreType.DMA((2,)),
        ],
        compiler_params=pltpu.CompilerParams(
            collective_id=0, has_side_effects=True, vmem_limit_bytes=60 << 20
        ),
        name="layer",
    )(amax_prior, tokens, out_grad, weights, down_weight)
    wide_top = peaks[4, 0] + 1e-6
    down_top = peaks[5, 0] + 1e-6
    gate_grad = (wide[:, :width].astype(F32) / wide_top).astype(BF)
    up_grad = (wide[:, width : 2 * width].astype(F32) / wide_top).astype(BF)
    down_grad = (wdown.astype(F32) / down_top).astype(BF)
    return (output, input_grad, gate_grad, up_grad, down_grad, peaks[8:14, 0])


def solution(mesh):
    placed = (
        P("hid", "tok"),
        P("tok", "hid"),
        P("tok", "hid"),
        P("hid", "tok"),
        P("hid", "tok"),
        P(),
    )
    return jax.shard_map(
        shards,
        mesh=mesh,
        in_specs=placed,
        out_specs=(
            P("hid", "tok"),
            P("hid", "tok"),
            P("tok", "hid"),
            P("tok", "hid"),
            P("hid", "tok"),
            P(),
        ),
        check_vma=False,
    )
```

```python
import jax
import jax.numpy as jnp
from jax import lax
from jax.experimental import pallas as pl
from jax.experimental.pallas import tpu as pltpu
from jax.sharding import PartitionSpec as P

MESH = pl.DeviceIdType.MESH
BF = jnp.bfloat16
F32 = jnp.float32
HALF = 1024
UNITS = 416
WIDE = 832


def contract_last(left, right):
    return lax.dot_general(left, right, (((1,), (1,)), ((), ())), preferred_element_type=F32)


def contract_first(left, right):
    return lax.dot_general(left, right, (((0,), (0,)), ((), ())), preferred_element_type=F32)


def quantize(value, scale):
    return jnp.clip(value / scale, -448.0, 448.0).astype(BF)


class Links:
    def __init__(self, send, recv):
        self.send, self.recv, self.used, self.open = send, recv, 0, []

    def slots(self, count):
        first = self.used
        self.used += count
        return first

    def copy(self, src, dst, slot, device):
        return pltpu.make_async_remote_copy(
            src_ref=src,
            dst_ref=dst,
            send_sem=self.send.at[slot],
            recv_sem=self.recv.at[slot],
            device_id=device,
            device_id_type=MESH,
        )

    def start(self, src, dst, slot, device):
        copy = self.copy(src, dst, slot, device)
        copy.start()
        self.open.append(copy)

    def arrived(self, dst, slot, device):
        self.copy(dst, dst, slot, device).wait_recv()

    def finish(self):
        for copy in self.open:
            copy.wait_send()


N_SEMS = 240


def kernel(
    prior, tokens, out_grad, gate_hbm, up_hbm, down_hbm,
    out_ref, in_grad_ref, wide_hbm, wdown_hbm, peaks_ref,
    xb, gb, wide_w, down_w, swap_out, swap_in,
    part, keep, got1, send2, got2,
    dpart, dkeep, dgot1, dsend2, dgot2,
    hb, db,
    o_refs, i_refs,
    wide_g, down_g, max_s, max_r,
    send_sem, recv_sem, load_sem, store_sem,
):
    t = lax.axis_index("tok")
    h = lax.axis_index("hid")
    y, zh, x, c = h // 16, (h // 8) % 2, (h // 2) % 4, h % 2
    p, s = t % 2, t // 2

    def device(dt=0, dy=0, dz=0, dx=0, dc=0):
        hid = ((((y + dy) % 4) * 2 + (zh + dz) % 2) * 4 + (x + dx) % 4) * 2 + (c + dc) % 2
        return ((t + dt) % 4, hid)

    def beside():
        return (t + 1 - 2 * p, h)

    peers = [device(dx=d, dc=e) for d in range(4) for e in range(2) if d or e]
    peers += [device(dy=d) for d in (1, 2, 3)]
    peers += [device(dt=d, dz=e) for d in range(4) for e in range(2) if d or e]
    barrier = pltpu.get_barrier_semaphore()
    for peer in peers:
        pl.semaphore_signal(barrier, inc=1, device_id=peer, device_id_type=MESH)

    loads = [
        pltpu.make_async_copy(gate_hbm, wide_w.at[pl.ds(0, UNITS)], load_sem.at[0]),
        pltpu.make_async_copy(up_hbm, wide_w.at[pl.ds(UNITS, UNITS)], load_sem.at[1]),
        pltpu.make_async_copy(down_hbm, down_w, load_sem.at[2]),
    ]
    for load in loads:
        load.start()

    s0, s1, s2, s3 = [prior[i] / 448.0 for i in range(4)]
    mine = pl.ds(pl.multiple_of(c * HALF, HALF), HALF)
    other = pl.ds(pl.multiple_of((1 - c) * HALF, HALF), HALF)

    tok_f = tokens[...].astype(F32)
    og_f = out_grad[...].astype(F32)
    max_x = jnp.max(jnp.abs(tok_f))
    max_g = jnp.max(jnp.abs(og_f))
    swap_out[pl.ds(0, 8), :] = quantize(tok_f, s0).astype(F32)
    swap_out[pl.ds(8, 8), :] = quantize(og_f, s2).astype(F32)

    links = Links(send_sem, recv_sem)
    core = device(dc=1)

    pl.semaphore_wait(barrier, len(peers))

    slot = links.slots(1)
    links.start(swap_out.at[:, other], swap_in, slot, core)
    links.arrived(swap_in, slot, core)
    own = swap_out[:, mine]
    theirs = swap_in[...]
    low = jnp.where(c == 0, own, theirs)
    high = jnp.where(c == 0, theirs, own)
    xb[y, zh, x, :, mine] = jnp.concatenate([low[0:8], high[0:8]], axis=0).astype(BF)
    gb[y, zh, x, :, mine] = jnp.concatenate([low[8:16], high[8:16]], axis=0).astype(BF)

    def step_x(d):
        return device(dx=d)

    def step_y(d):
        return device(dy=d)

    away = device(dz=1)
    cols_xy = pl.ds(pl.multiple_of(c * HALF, 512), 512)
    cols_yx = pl.ds(pl.multiple_of(c * HALF + 512, 512), 512)

    class Gather:
        def __init__(self, buf):
            self.buf = buf
            self.z = links.slots(1)
            self.first = {a: (links.slots(4), links.slots(4)) for a in (0, 1)}
            self.second = {a: (links.slots(4), links.slots(4)) for a in (0, 1)}
            self.swap = (links.slots(4), links.slots(4))

        def level(self, a):
            return zh if a == 0 else 1 - zh

        def send_z(self):
            block = self.buf.at[y, zh, x, :, mine]
            links.start(block, block, self.z, away)

        def wait_z(self):
            links.arrived(self.buf.at[y, 1 - zh, x, :, mine], self.z, away)

        def send_first(self, a):
            z = self.level(a)
            for d in (1, 3, 2):
                block = self.buf.at[y, z, x, :, cols_xy]
                links.start(block, block, self.first[a][0] + d, step_x(d))
                block = self.buf.at[y, z, x, :, cols_yx]
                links.start(block, block, self.first[a][1] + d, step_y(d))

        def wait_first(self, a):
            z = self.level(a)
            for d in (1, 3, 2):
                block = self.buf.at[y, z, (x - d) % 4, :, cols_xy]
                links.arrived(block, self.first[a][0] + d, step_x(4 - d))
                block = self.buf.at[(y - d) % 4, z, x, :, cols_yx]
                links.arrived(block, self.first[a][1] + d, step_y(4 - d))

        def send_second(self, a):
            z = self.level(a)
            for d in (1, 3, 2):
                rows = self.buf.at[y, z, :, :, cols_xy]
                links.start(rows, rows, self.second[a][0] + d, step_y(d))
                rows = self.buf.at[:, z, x, :, cols_yx]
                links.start(rows, rows, self.second[a][1] + d, step_x(d))

        def wait_second(self, d):
            for a in (0, 1):
                z = self.level(a)
                rows = self.buf.at[(y - d) % 4, z, :, :, cols_xy]
                links.arrived(rows, self.second[a][0] + d, step_y(4 - d))
                rows = self.buf.at[:, z, (x - d) % 4, :, cols_yx]
                links.arrived(rows, self.second[a][1] + d, step_x(4 - d))

        def send_swap(self, d):
            rows = self.buf.at[(y - d) % 4, :, :, :, cols_xy]
            links.start(rows, rows, self.swap[0] + d, core)
            rows = self.buf.at[:, :, (x - d) % 4, :, cols_yx]
            links.start(rows, rows, self.swap[1] + d, core)

        def wait_swap(self):
            there_xy = pl.ds(pl.multiple_of((1 - c) * HALF, 512), 512)
            there_yx = pl.ds(pl.multiple_of((1 - c) * HALF + 512, 512), 512)
            for d in (0, 1, 3, 2):
                rows = self.buf.at[(y - d) % 4, :, :, :, there_xy]
                links.arrived(rows, self.swap[0] + d, core)
                rows = self.buf.at[:, :, (x - d) % 4, :, there_yx]
                links.arrived(rows, self.swap[1] + d, core)

    gx, gg = Gather(xb), Gather(gb)
    gx.send_z()
    gx.send_first(0)
    gg.send_z()
    gg.send_first(0)
    gx.wait_z()
    gx.send_first(1)
    gg.wait_z()
    gg.send_first(1)
    for gather in (gx, gg):
        gather.wait_first(0)
        gather.send_second(0)
        gather.wait_first(1)
        gather.send_second(1)
        gather.send_swap(0)
    for load in loads:
        load.wait()
    for d in (1, 3, 2):
        gx.wait_second(d)
        gx.send_swap(d)
    gx.wait_swap()

    order = ((1 - p) + 2 * (1 - s), (1 - p) + 2 * s, p + 2 * (1 - s), p + 2 * s)
    r1, r2 = links.slots(4), links.slots(2)
    d1, d2 = links.slots(2), links.slots(1)
    partner = beside()
    far = device(dt=2)
    units = (pl.ds(0, UNITS), pl.ds(UNITS, UNITS))

    def pair(buf, j):
        two = [buf[(y + k) % 4].reshape(128, 2048) for k in order[j : j + 2]]
        return jnp.concatenate(two, axis=0)

    value = contract_last(wide_w[...], pair(xb, 0))
    for j, to in ((0, 1 - s), (1, s)):
        part[j] = value[:, 128 * j : 128 * j + 128].astype(BF)
        for u in (0, 1):
            links.start(part.at[j, units[u]], got1.at[to, units[u]], r1 + 2 * to + u, partner)
    value = contract_last(wide_w[...], pair(xb, 2))
    keep[0] = value[:, :128]
    keep[1] = value[:, 128:]
    for d in (1, 3, 2):
        gg.wait_second(d)
        gg.send_swap(d)
    gg.wait_swap()
    value = contract_last(down_w[...], pair(gb, 0))
    for j, to in ((0, 1 - s), (1, s)):
        dpart[j] = value[:, 128 * j : 128 * j + 128].astype(BF)
        links.start(dpart.at[j], dgot1.at[to], d1 + to, partner)
    value = contract_last(down_w[...], pair(gb, 2))
    dkeep[0] = value[:, :128]
    dkeep[1] = value[:, 128:]
    for u in (0, 1):
        links.arrived(got1.at[1 - s, units[u]], r1 + 2 * (1 - s) + u, partner)
        send2[units[u], :] = (keep[0, units[u]] + got1[1 - s, units[u]].astype(F32)).astype(BF)
        links.start(send2.at[units[u]], got2.at[units[u]], r2 + u, far)
    links.arrived(dgot1.at[1 - s], d1 + (1 - s), partner)
    dsend2[...] = (dkeep[0] + dgot1[1 - s].astype(F32)).astype(BF)
    links.start(dsend2, dgot2, d2, far)
    yt = (y + t) % 4
    h1, h2, h3 = links.slots(1), links.slots(1), links.slots(1)
    g1, g2, g3 = links.slots(2), links.slots(2), links.slots(2)

    for u in (0, 1):
        links.arrived(got1.at[s, units[u]], r1 + 2 * s + u, partner)
        links.arrived(got2.at[units[u]], r2 + u, far)
    both = (keep[1] + got1[s].astype(F32) + got2[...].astype(F32)) * s0
    gate = both[:UNITS]
    up = both[UNITS:]
    sig = jax.nn.sigmoid(gate)
    act = gate * sig
    hidden = act * up
    max_h = jnp.max(jnp.abs(hidden))
    hb[yt] = quantize(hidden, s1)
    links.start(hb.at[yt], hb.at[yt], h1, far)
    links.start(hb.at[yt], hb.at[yt], h2, partner)

    links.arrived(dgot1.at[s], d1 + s, partner)
    links.arrived(dgot2, d2, far)
    dhidden = (dkeep[1] + dgot1[s].astype(F32) + dgot2[...].astype(F32)) * s2
    dgate = dhidden * up * sig * (1.0 + gate * (1.0 - sig))
    dup = dhidden * act
    max_p = jnp.maximum(jnp.max(jnp.abs(dgate)), jnp.max(jnp.abs(dup)))
    for u, value in ((0, dgate), (1, dup)):
        db[yt, units[u]] = quantize(value, s3)
        links.start(db.at[yt, units[u]], db.at[yt, units[u]], g1 + u, far)
    for u in (0, 1):
        links.start(db.at[yt, units[u]], db.at[yt, units[u]], g2 + u, partner)
    yf = (y + (t + 2) % 4) % 4
    yp = (y + partner[0]) % 4
    ypf = (y + (partner[0] + 2) % 4) % 4
    links.arrived(hb.at[yf], h1, far)
    links.start(hb.at[yf], hb.at[yf], h3, partner)

    class Spread:
        def __init__(self, part, core_in, ring_y, ring_x, then_x, then_y, got_x, got_y, zs, zr, fin, fr):
            self.part, self.core_in, self.ring_y, self.ring_x = part, core_in, ring_y, ring_x
            self.then_x, self.then_y, self.got_x, self.got_y = then_x, then_y, got_x, got_y
            self.zs, self.zr, self.fin, self.fr = zs, zr, fin, fr
            self.cores, self.yx, self.xy = links.slots(4), links.slots(4), links.slots(16)
            self.x, self.y, self.z, self.c = links.slots(4), links.slots(4), links.slots(1), links.slots(1)

        def block(self, n, left, right):
            value = contract_first(left, right)
            at = blocks[n]
            self.part[at] = value.astype(BF).reshape(2, 4, 16, 2048)
            links.start(self.part.at[at, :, :, :, other], self.core_in.at[at], self.cores + n, core)

        def first(self, n):
            at, d = blocks[n], steps[n]
            links.arrived(self.core_in.at[at], self.cores + n, core)
            value = self.part[at, :, :, :, mine].astype(F32) + self.core_in[at].astype(F32)
            self.core_in[at] = value.astype(BF)

            @pl.when(d != 0)
            def _():
                src = self.core_in.at[at, :, :, :, left]
                links.copy(src, self.ring_y.at[d - 1], self.yx + d, device(dy=d)).start()

            for e in (1, 3, 2):
                src = self.core_in.at[at, :, (x + e) % 4, :, right]
                links.start(src, self.ring_x.at[e - 1, at], self.xy + 4 * n + e, step_x(e))

        def second(self):
            for d in (1, 3, 2):
                links.arrived(self.ring_y.at[d - 1], self.yx + d, step_y(4 - d))
            total = self.core_in[y, :, :, :, left].astype(F32)
            for d in (1, 2, 3):
                total = total + self.ring_y[d - 1].astype(F32)
            self.then_x[...] = total.astype(BF)
            for d in (1, 3, 2):
                links.start(self.then_x.at[:, (x + d) % 4], self.got_x.at[d - 1], self.x + d, step_x(d))
            for n in range(4):
                for e in (1, 3, 2):
                    links.arrived(self.ring_x.at[e - 1, blocks[n]], self.xy + 4 * n + e, step_x(4 - e))
            total = self.core_in[:, :, x, :, right].astype(F32)
            for d in (1, 2, 3):
                total = total + self.ring_x[d - 1].astype(F32)
            self.then_y[...] = total.astype(BF)
            for d in (1, 3, 2):
                links.start(self.then_y.at[(y + d) % 4], self.got_y.at[d - 1], self.y + d, step_y(d))

        def third(self):
            for d in (1, 3, 2):
                links.arrived(self.got_x.at[d - 1], self.x + d, step_x(4 - d))
            total = self.then_x[:, x].astype(F32)
            for d in (1, 2, 3):
                total = total + self.got_x[d - 1].astype(F32)
            self.zs[:, :, left] = total
            for d in (1, 3, 2):
                links.arrived(self.got_y.at[d - 1], self.y + d, step_y(4 - d))
            total = self.then_y[y].astype(F32)
            for d in (1, 2, 3):
                total = total + self.got_y[d - 1].astype(F32)
            self.zs[:, :, right] = total
            links.start(self.zs.at[1 - zh], self.zr, self.z, away)

        def fourth(self):
            links.arrived(self.zr, self.z, away)
            self.fin[...] = self.zs[zh] + self.zr[...]
            links.start(self.fin.at[rows_other], self.fr, self.c, core)

        def last(self, ref, scale):
            links.arrived(self.fr, self.c, core)
            ref[:, mine] = (self.fin[rows_mine, :] * scale).astype(BF)
            ref[:, other] = (self.fr[...] * scale).astype(BF)

        def finish(self):
            for d in (1, 2, 3):
                src = self.core_in.at[0, :, :, :, left]
                links.copy(src, self.ring_y.at[0], self.yx + d, step_y(d)).wait_send()

    left, right = pl.ds(0, 512), pl.ds(512, 512)
    rows_other = pl.ds(pl.multiple_of((1 - c) * 8, 8), 8)
    rows_mine = pl.ds(pl.multiple_of(c * 8, 8), 8)
    steps = (t, (t + 2) % 4, partner[0], (partner[0] + 2) % 4)
    blocks = (yt, yf, yp, ypf)
    out_sum = Spread(*o_refs)
    in_sum = Spread(*i_refs)

    for n in (0, 1):
        out_sum.block(n, hb[blocks[n]], down_w[...])
    links.arrived(hb.at[yp], h2, partner)
    out_sum.block(2, hb[yp], down_w[...])
    links.arrived(hb.at[ypf], h3, partner)
    out_sum.block(3, hb[ypf], down_w[...])
    for n in range(4):
        out_sum.first(n)

    def pass_on():
        for u in (0, 1):
            links.arrived(db.at[yf, units[u]], g1 + u, far)
            links.start(db.at[yf, units[u]], db.at[yf, units[u]], g3 + u, partner)

    hq_all = jnp.concatenate([hb[n] for n in range(4)], axis=1)

    def down_tile(i, top):
        columns = pl.ds(pl.multiple_of(i * 256, 256), 256)
        rows = gb[:, :, :, :, columns].reshape(512, 256)
        value = jnp.dot(hq_all, rows, preferred_element_type=F32) * (s1 * s2)
        down_g[:, columns] = value.astype(BF)
        return jnp.maximum(top, jnp.max(jnp.abs(value)))

    max_d = lax.fori_loop(0, 4, down_tile, jnp.float32(0.0))
    pass_on()
    in_sum.block(0, db[yt], wide_w[...])
    in_sum.block(1, db[yf], wide_w[...])
    out_sum.second()
    max_d = lax.fori_loop(4, 8, down_tile, max_d)
    store_d = pltpu.make_async_copy(down_g, wdown_hbm, store_sem.at[0])
    store_d.start()
    in_sum.first(0)
    in_sum.first(1)
    for u in (0, 1):
        links.arrived(db.at[yp, units[u]], g2 + u, partner)
    in_sum.block(2, db[yp], wide_w[...])
    out_sum.third()
    for u in (0, 1):
        links.arrived(db.at[ypf, units[u]], g3 + u, partner)
    in_sum.block(3, db[ypf], wide_w[...])

    dq_all = jnp.concatenate([db[n] for n in range(4)], axis=1)

    def wide_tile(i, top):
        columns = pl.ds(pl.multiple_of(i * 256, 256), 256)
        rows = xb[:, :, :, :, columns].reshape(512, 256)
        value = jnp.dot(dq_all, rows, preferred_element_type=F32) * (s0 * s3)
        wide_g[:, columns] = value.astype(BF)
        return jnp.maximum(top, jnp.max(jnp.abs(value)))

    in_sum.first(2)
    max_w = lax.fori_loop(0, 2, wide_tile, jnp.float32(0.0))
    in_sum.first(3)
    max_w = lax.fori_loop(2, 8, wide_tile, max_w)
    store_w = pltpu.make_async_copy(wide_g, wide_hbm, store_sem.at[1])
    store_w.start()

    row = lax.broadcasted_iota(jnp.int32, (8, 128), 0)
    tops = jnp.zeros((8, 128), F32)
    for n, value in enumerate((max_x, max_h, max_g, max_p, max_w, max_d)):
        tops = jnp.where(row == n, value, tops)

    def send_tops(stage, value, offsets):
        first = links.slots(len(offsets))
        max_s[stage] = value
        for n, offset in enumerate(offsets):
            links.start(max_s.at[stage], max_r.at[stage, n], first + n, device(**offset))
        return first

    def take_tops(stage, value, offsets, first):
        for n, offset in enumerate(offsets):
            back = {name: -d for name, d in offset.items()}
            links.arrived(max_r.at[stage, n], first + n, device(**back))
            value = jnp.maximum(value, max_r[stage, n])
        return value

    plane = [dict(dx=d, dc=e) for d in range(4) for e in range(2) if d or e]
    depth = [dict(dt=d, dz=e) for d in range(4) for e in range(2) if d or e]
    column = [dict(dy=d) for d in (1, 2, 3)]
    first = send_tops(0, tops, plane)
    in_sum.second()
    tops = take_tops(0, tops, plane, first)
    first = send_tops(1, tops, column)
    out_sum.fourth()
    in_sum.third()
    tops = take_tops(1, tops, column, first)
    first = send_tops(2, tops, depth)
    out_sum.last(out_ref, s1)
    in_sum.fourth()
    tops = take_tops(2, tops, depth, first)
    peaks_ref[pl.ds(0, 8), :] = tops
    peaks_ref[pl.ds(8, 8), :] = jnp.log(tops + 1e-6)
    in_sum.last(in_grad_ref, s3)

    out_sum.finish()
    in_sum.finish()
    links.finish()
    store_d.wait()
    store_w.wait()
    assert links.used <= N_SEMS


def scale_grads(
    peaks, out_in, in_grad_in, wide_hbm, wdown_hbm,
    gate_out, up_out, down_out, out_ref, in_grad_ref, amaxes_ref,
    held, scaled, load_sem, store_sem,
):
    size = UNITS // 2
    halves = [pl.ds(n * size, size) for n in range(4)]
    sources = [wide_hbm.at[rows] for rows in halves] + [wdown_hbm.at[rows] for rows in halves[:2]]
    targets = [ref.at[rows] for ref in (gate_out, up_out, down_out) for rows in halves[:2]]
    loads = [
        pltpu.make_async_copy(source, held.at[n], load_sem.at[n]) for n, source in enumerate(sources)
    ]
    stores = [
        pltpu.make_async_copy(scaled.at[n], target, store_sem.at[n])
        for n, target in enumerate(targets)
    ]
    for load in loads:
        load.start()
    for n in range(6):
        amaxes_ref[n] = peaks[8 + n, 0]
    out_ref[...] = out_in[...]
    in_grad_ref[...] = in_grad_in[...]
    over_wide = 1.0 / (peaks[4, 0] + 1e-6)
    over_down = 1.0 / (peaks[5, 0] + 1e-6)
    for n in range(6):
        loads[n].wait()
        over = over_wide if n < 4 else over_down
        scaled[n] = (held[n].astype(F32) * over).astype(BF)
        stores[n].start()
    for store in stores:
        store.wait()


def shards(tokens, gate_weight, up_weight, down_weight, out_grad, amax_prior):
    vmem = pl.BlockSpec(memory_space=pltpu.VMEM)
    hbm = pl.BlockSpec(memory_space=pl.ANY)
    V = pltpu.VMEM
    sum_scratch = (
        V((4, 2, 4, 16, 2048), BF), V((4, 2, 4, 16, HALF), BF),
        V((3, 2, 4, 16, 512), BF), V((3, 4, 2, 16, 512), BF),
        V((2, 4, 16, 512), BF), V((4, 2, 16, 512), BF),
        V((3, 2, 16, 512), BF), V((3, 2, 16, 512), BF),
        V((2, 16, HALF), F32), V((16, HALF), F32), V((16, HALF), F32), V((8, HALF), F32),
    )
    output, input_grad, wide, wdown, peaks = pl.pallas_call(
        kernel,
        out_shape=(
            jax.ShapeDtypeStruct((8, 2048), BF),
            jax.ShapeDtypeStruct((8, 2048), BF),
            jax.ShapeDtypeStruct((WIDE, 2048), BF),
            jax.ShapeDtypeStruct((UNITS, 2048), BF),
            jax.ShapeDtypeStruct((16, 128), F32),
        ),
        in_specs=[pl.BlockSpec(memory_space=pltpu.SMEM), vmem, vmem, hbm, hbm, hbm],
        out_specs=(vmem, vmem, hbm, hbm, vmem),
        scratch_shapes=[
            V((4, 2, 4, 16, 2048), BF), V((4, 2, 4, 16, 2048), BF),
            V((WIDE, 2048), BF), V((UNITS, 2048), BF),
            V((16, 2048), F32), V((16, HALF), F32),
            V((2, WIDE, 128), BF), V((2, WIDE, 128), F32), V((2, WIDE, 128), BF),
            V((WIDE, 128), BF), V((WIDE, 128), BF),
            V((2, UNITS, 128), BF), V((2, UNITS, 128), F32), V((2, UNITS, 128), BF),
            V((UNITS, 128), BF), V((UNITS, 128), BF),
            V((4, UNITS, 128), BF), V((4, WIDE, 128), BF),
            sum_scratch, sum_scratch,
            V((WIDE, 2048), BF), V((UNITS, 2048), BF),
            V((3, 8, 128), F32), V((3, 7, 8, 128), F32),
            pltpu.SemaphoreType.DMA((N_SEMS,)), pltpu.SemaphoreType.DMA((N_SEMS,)),
            pltpu.SemaphoreType.DMA((3,)), pltpu.SemaphoreType.DMA((2,)),
        ],
        compiler_params=pltpu.CompilerParams(
            collective_id=0, has_side_effects=True, vmem_limit_bytes=60 << 20
        ),
        name="layer",
    )(amax_prior, tokens, out_grad, gate_weight.T, up_weight.T, down_weight)
    full = (
        jax.ShapeDtypeStruct((UNITS, 2048), BF),
        jax.ShapeDtypeStruct((UNITS, 2048), BF),
        jax.ShapeDtypeStruct((UNITS, 2048), BF),
        jax.ShapeDtypeStruct((8, 2048), BF),
        jax.ShapeDtypeStruct((8, 2048), BF),
        jax.ShapeDtypeStruct((6,), F32),
    )
    smem = pl.BlockSpec(memory_space=pltpu.SMEM)
    gate_grad, up_grad, down_grad, output, input_grad, amaxes = pl.pallas_call(
        scale_grads,
        out_shape=full,
        in_specs=[smem, vmem, vmem, hbm, hbm],
        out_specs=(hbm, hbm, hbm, vmem, vmem, smem),
        scratch_shapes=[
            V((6, UNITS // 2, 2048), BF),
            V((6, UNITS // 2, 2048), BF),
            pltpu.SemaphoreType.DMA((6,)),
            pltpu.SemaphoreType.DMA((6,)),
        ],
        compiler_params=pltpu.CompilerParams(vmem_limit_bytes=60 << 20),
        name="scale",
    )(peaks, output, input_grad, wide, wdown)
    return (output, input_grad, gate_grad.T, up_grad.T, down_grad, amaxes)


def solution(mesh):
    placed = (
        P("hid", "tok"),
        P("tok", "hid"),
        P("tok", "hid"),
        P("hid", "tok"),
        P("hid", "tok"),
        P(),
    )
    return jax.shard_map(
        shards,
        mesh=mesh,
        in_specs=placed,
        out_specs=(
            P("hid", "tok"),
            P("hid", "tok"),
            P("tok", "hid"),
            P("tok", "hid"),
            P("hid", "tok"),
            P(),
        ),
        check_vma=False,
    )
```

```python
import jax
import jax.numpy as jnp
from jax import lax
from jax.experimental import pallas as pl
from jax.experimental.pallas import tpu as pltpu
from jax.sharding import PartitionSpec as P

MESH = pl.DeviceIdType.MESH
BF = jnp.bfloat16
F32 = jnp.float32
HALF = 1024
UNITS = 416
WIDE = 832


def contract_last(left, right):
    return lax.dot_general(left, right, (((1,), (1,)), ((), ())), preferred_element_type=F32)


def contract_first(left, right):
    return lax.dot_general(left, right, (((0,), (0,)), ((), ())), preferred_element_type=F32)


def quantize(value, scale):
    return jnp.clip(value / scale, -448.0, 448.0).astype(BF)


class Links:
    def __init__(self, send, recv):
        self.send, self.recv, self.used, self.open = send, recv, 0, []

    def slots(self, count):
        first = self.used
        self.used += count
        return first

    def copy(self, src, dst, slot, device):
        return pltpu.make_async_remote_copy(
            src_ref=src,
            dst_ref=dst,
            send_sem=self.send.at[slot],
            recv_sem=self.recv.at[slot],
            device_id=device,
            device_id_type=MESH,
        )

    def start(self, src, dst, slot, device):
        copy = self.copy(src, dst, slot, device)
        copy.start()
        self.open.append(copy)

    def arrived(self, dst, slot, device):
        self.copy(dst, dst, slot, device).wait_recv()

    def finish(self):
        for copy in self.open:
            copy.wait_send()


N_SEMS = 260


def kernel(
    prior, tokens, out_grad, gate_hbm, up_hbm, down_hbm,
    out_ref, in_grad_ref, wide_hbm, wdown_hbm, peaks_ref,
    xb, gb, wide_w, down_w, swap_out, swap_in,
    part, keep, got1, send2, got2,
    dpart, dkeep, dgot1, dsend2, dgot2,
    hb, db,
    o_refs, i_refs,
    wide_g, down_g, max_s, max_r,
    send_sem, recv_sem, load_sem, store_sem,
):
    t = lax.axis_index("tok")
    h = lax.axis_index("hid")
    y, zh, x, c = h // 16, (h // 8) % 2, (h // 2) % 4, h % 2
    p, s = t % 2, t // 2

    def device(dt=0, dy=0, dz=0, dx=0, dc=0):
        hid = ((((y + dy) % 4) * 2 + (zh + dz) % 2) * 4 + (x + dx) % 4) * 2 + (c + dc) % 2
        return ((t + dt) % 4, hid)

    def beside():
        return (t + 1 - 2 * p, h)

    peers = [device(dx=d, dc=e) for d in range(4) for e in range(2) if d or e]
    peers += [device(dy=d) for d in (1, 2, 3)]
    peers += [device(dt=d, dz=e) for d in range(4) for e in range(2) if d or e]
    peers += [device(dz=1, dc=1)]
    barrier = pltpu.get_barrier_semaphore()
    for peer in peers:
        pl.semaphore_signal(barrier, inc=1, device_id=peer, device_id_type=MESH)

    loads = [
        pltpu.make_async_copy(gate_hbm, wide_w.at[pl.ds(0, UNITS)], load_sem.at[0]),
        pltpu.make_async_copy(up_hbm, wide_w.at[pl.ds(UNITS, UNITS)], load_sem.at[1]),
        pltpu.make_async_copy(down_hbm, down_w, load_sem.at[2]),
    ]
    for load in loads:
        load.start()

    s0, s1, s2, s3 = [prior[i] / 448.0 for i in range(4)]
    mine = pl.ds(pl.multiple_of(c * HALF, HALF), HALF)
    other = pl.ds(pl.multiple_of((1 - c) * HALF, HALF), HALF)

    tok_f = tokens[...].astype(F32)
    og_f = out_grad[...].astype(F32)
    max_x = jnp.max(jnp.abs(tok_f))
    max_g = jnp.max(jnp.abs(og_f))
    swap_out[...] = jnp.concatenate(
        [quantize(tok_f, s0).astype(F32), quantize(og_f, s2).astype(F32)], axis=0
    ).astype(BF)

    links = Links(send_sem, recv_sem)
    core = device(dc=1)

    pl.semaphore_wait(barrier, len(peers))

    first = links.slots(3)
    away = device(dz=1)
    across = device(dz=1, dc=1)
    links.start(swap_out.at[:, mine], swap_in.at[1], first + 1, away)
    links.start(swap_out.at[:, other], swap_in.at[2], first + 2, across)
    links.start(swap_out.at[:, other], swap_in.at[0], first, core)

    def place(z, own, theirs):
        own, theirs = own.astype(F32), theirs.astype(F32)
        low = jnp.where(c == 0, own, theirs)
        high = jnp.where(c == 0, theirs, own)
        xb[y, z, x, :, mine] = jnp.concatenate([low[0:8], high[0:8]], axis=0).astype(BF)
        gb[y, z, x, :, mine] = jnp.concatenate([low[8:16], high[8:16]], axis=0).astype(BF)

    links.arrived(swap_in.at[0], first, core)
    place(zh, swap_out[:, mine], swap_in[0])
    def step_x(d):
        return device(dx=d)

    def step_y(d):
        return device(dy=d)

    cols_xy = pl.ds(pl.multiple_of(c * HALF, 512), 512)
    cols_yx = pl.ds(pl.multiple_of(c * HALF + 512, 512), 512)

    class Gather:
        def __init__(self, buf):
            self.buf = buf
            self.first = {a: (links.slots(4), links.slots(4)) for a in (0, 1)}
            self.second = {a: (links.slots(4), links.slots(4)) for a in (0, 1)}
            self.swap = {a: (links.slots(4), links.slots(4)) for a in (0, 1)}

        def level(self, a):
            return zh if a == 0 else 1 - zh

        def send_first(self, a):
            z = self.level(a)
            for d in (1, 3, 2):
                block = self.buf.at[y, z, x, :, cols_xy]
                links.start(block, block, self.first[a][0] + d, step_x(d))
                block = self.buf.at[y, z, x, :, cols_yx]
                links.start(block, block, self.first[a][1] + d, step_y(d))

        def wait_first(self, a):
            z = self.level(a)
            for d in (1, 3, 2):
                block = self.buf.at[y, z, (x - d) % 4, :, cols_xy]
                links.arrived(block, self.first[a][0] + d, step_x(4 - d))
                block = self.buf.at[(y - d) % 4, z, x, :, cols_yx]
                links.arrived(block, self.first[a][1] + d, step_y(4 - d))

        def send_second(self, a):
            z = self.level(a)
            for d in (1, 3, 2):
                rows = self.buf.at[y, z, :, :, cols_xy]
                links.start(rows, rows, self.second[a][0] + d, step_y(d))
                rows = self.buf.at[:, z, x, :, cols_yx]
                links.start(rows, rows, self.second[a][1] + d, step_x(d))

        def wait_second(self, a, d):
            z = self.level(a)
            rows = self.buf.at[(y - d) % 4, z, :, :, cols_xy]
            links.arrived(rows, self.second[a][0] + d, step_y(4 - d))
            rows = self.buf.at[:, z, (x - d) % 4, :, cols_yx]
            links.arrived(rows, self.second[a][1] + d, step_x(4 - d))

        def send_swap(self, a, d):
            z = self.level(a)
            rows = self.buf.at[(y - d) % 4, z, :, :, cols_xy]
            links.start(rows, rows, self.swap[a][0] + d, core)
            rows = self.buf.at[:, z, (x - d) % 4, :, cols_yx]
            links.start(rows, rows, self.swap[a][1] + d, core)

        def wait_swap(self, a):
            z = self.level(a)
            there_xy = pl.ds(pl.multiple_of((1 - c) * HALF, 512), 512)
            there_yx = pl.ds(pl.multiple_of((1 - c) * HALF + 512, 512), 512)
            for d in (0, 1, 3, 2):
                rows = self.buf.at[(y - d) % 4, z, :, :, there_xy]
                links.arrived(rows, self.swap[a][0] + d, core)
                rows = self.buf.at[:, z, (x - d) % 4, :, there_yx]
                links.arrived(rows, self.swap[a][1] + d, core)

        def complete(self, a):
            for d in (1, 3, 2):
                self.wait_second(a, d)
                self.send_swap(a, d)
            self.wait_swap(a)

    gx, gg = Gather(xb), Gather(gb)
    gx.send_first(0)
    gg.send_first(0)
    gx.wait_first(0)
    gx.send_second(0)
    links.arrived(swap_in.at[1], first + 1, away)
    links.arrived(swap_in.at[2], first + 2, across)
    place(1 - zh, swap_in[1], swap_in[2])
    gx.send_first(1)
    gg.send_first(1)
    gx.send_swap(0, 0)
    gg.wait_first(0)
    gg.send_second(0)
    gx.wait_first(1)
    gx.send_second(1)
    gg.wait_first(1)
    gg.send_second(1)
    gx.send_swap(1, 0)
    gg.send_swap(0, 0)
    gg.send_swap(1, 0)
    for load in loads:
        load.wait()
    gx.complete(0)

    order = ((1 - p) + 2 * (1 - s), (1 - p) + 2 * s, p + 2 * (1 - s), p + 2 * s)
    r1, r2 = links.slots(4), links.slots(2)
    d1, d2 = links.slots(2), links.slots(1)
    partner = beside()
    far = device(dt=2)
    units = (pl.ds(0, UNITS), pl.ds(UNITS, UNITS))
    lower = lax.broadcasted_iota(jnp.int32, (UNITS, 128), 1) < 64

    def turn(value):
        return pltpu.roll(value, 64, 1)

    def pair(buf, j, z=None):
        two = [buf[(y + k) % 4] if z is None else buf[(y + k) % 4, z] for k in order[j : j + 2]]
        return jnp.concatenate([value.reshape(-1, 2048) for value in two], axis=0)

    def gate_and_up(j, z):
        value = contract_last(wide_w[...], pair(xb, j, z))
        gate, up = value[:UNITS], value[UNITS:]
        return jnp.where(lower, gate, turn(up)), jnp.where(lower, turn(gate), up)

    for a, z in ((0, zh), (1, 1 - zh)):
        if a:
            gx.complete(1)
        for j, to, value in zip((0, 1), (1 - s, s), gate_and_up(0, z)):
            part[j, a] = value.astype(BF)
            links.start(part.at[j, a], got1.at[to, z], r1 + 2 * to + a, partner)
        for j, value in zip((0, 1), gate_and_up(2, z)):
            keep[j, z] = value

    def send_far(a, z):
        links.arrived(got1.at[1 - s, z], r1 + 2 * (1 - s) + a, partner)
        send2[z] = (keep[0, z] + got1[1 - s, z].astype(F32)).astype(BF)
        links.start(send2.at[z], got2.at[z], r2 + a, far)

    send_far(0, zh)
    gg.complete(0)
    gg.complete(1)
    value = contract_last(down_w[...], pair(gb, 0))
    for j, to in ((0, 1 - s), (1, s)):
        dpart[j] = value[:, 128 * j : 128 * j + 128].astype(BF)
        links.start(dpart.at[j], dgot1.at[to], d1 + to, partner)
    value = contract_last(down_w[...], pair(gb, 2))
    dkeep[0] = value[:, :128]
    dkeep[1] = value[:, 128:]
    send_far(1, 1 - zh)
    links.arrived(dgot1.at[1 - s], d1 + (1 - s), partner)
    dsend2[...] = (dkeep[0] + dgot1[1 - s].astype(F32)).astype(BF)
    links.start(dsend2, dgot2, d2, far)
    yt = (y + t) % 4
    h1, h2, h3 = links.slots(1), links.slots(1), links.slots(1)
    g1, g2, g3 = links.slots(2), links.slots(2), links.slots(2)

    for a, z in ((0, zh), (1, 1 - zh)):
        links.arrived(got1.at[s, z], r1 + 2 * s + a, partner)
        links.arrived(got2.at[z], r2 + a, far)
    low, high = [
        (keep[1, z] + got1[s, z].astype(F32) + got2[z].astype(F32)) * s0 for z in (0, 1)
    ]
    gate = jnp.where(lower, low, turn(high))
    up = jnp.where(lower, turn(low), high)
    sig = jax.nn.sigmoid(gate)
    act = gate * sig
    hidden = act * up
    max_h = jnp.max(jnp.abs(hidden))
    hb[yt] = quantize(hidden, s1)
    links.start(hb.at[yt], hb.at[yt], h1, far)
    links.start(hb.at[yt], hb.at[yt], h2, partner)

    links.arrived(dgot1.at[s], d1 + s, partner)
    links.arrived(dgot2, d2, far)
    dhidden = (dkeep[1] + dgot1[s].astype(F32) + dgot2[...].astype(F32)) * s2
    dgate = dhidden * up * sig * (1.0 + gate * (1.0 - sig))
    dup = dhidden * act
    max_p = jnp.maximum(jnp.max(jnp.abs(dgate)), jnp.max(jnp.abs(dup)))
    for u, value in ((0, dgate), (1, dup)):
        db[yt, units[u]] = quantize(value, s3)
        links.start(db.at[yt, units[u]], db.at[yt, units[u]], g1 + u, far)
    for u in (0, 1):
        links.start(db.at[yt, units[u]], db.at[yt, units[u]], g2 + u, partner)
    yf = (y + (t + 2) % 4) % 4
    yp = (y + partner[0]) % 4
    ypf = (y + (partner[0] + 2) % 4) % 4
    links.arrived(hb.at[yf], h1, far)
    links.start(hb.at[yf], hb.at[yf], h3, partner)

    class Spread:
        def __init__(self, part, core_in, ring_y, ring_x, then_x, then_y, got_x, got_y, zs, fr):
            self.part, self.core_in, self.ring_y, self.ring_x = part, core_in, ring_y, ring_x
            self.then_x, self.then_y, self.got_x, self.got_y = then_x, then_y, got_x, got_y
            self.zs, self.fr = zs, fr
            self.cores, self.yx, self.xy = links.slots(4), links.slots(4), links.slots(16)
            self.x, self.y, self.z = links.slots(4), links.slots(4), links.slots(3)

        def block(self, n, left, right):
            value = contract_first(left, right)
            at = blocks[n]
            self.part[at] = value.astype(BF).reshape(2, 4, 16, 2048)
            links.start(self.part.at[at, :, :, :, other], self.core_in.at[at], self.cores + n, core)

        def first(self, n):
            at, d = blocks[n], steps[n]
            links.arrived(self.core_in.at[at], self.cores + n, core)
            value = self.part[at, :, :, :, mine].astype(F32) + self.core_in[at].astype(F32)
            self.core_in[at] = value.astype(BF)

            @pl.when(d != 0)
            def _():
                src = self.core_in.at[at, :, :, :, left]
                links.copy(src, self.ring_y.at[d - 1], self.yx + d, device(dy=d)).start()

            for e in (1, 3, 2):
                src = self.core_in.at[at, :, (x + e) % 4, :, right]
                links.start(src, self.ring_x.at[e - 1, at], self.xy + 4 * n + e, step_x(e))

        def second(self):
            for d in (1, 3, 2):
                links.arrived(self.ring_y.at[d - 1], self.yx + d, step_y(4 - d))
            total = self.core_in[y, :, :, :, left].astype(F32)
            for d in (1, 2, 3):
                total = total + self.ring_y[d - 1].astype(F32)
            self.then_x[...] = total.astype(BF)
            for d in (1, 3, 2):
                links.start(self.then_x.at[:, (x + d) % 4], self.got_x.at[d - 1], self.x + d, step_x(d))
            for n in range(4):
                for e in (1, 3, 2):
                    links.arrived(self.ring_x.at[e - 1, blocks[n]], self.xy + 4 * n + e, step_x(4 - e))
            total = self.core_in[:, :, x, :, right].astype(F32)
            for d in (1, 2, 3):
                total = total + self.ring_x[d - 1].astype(F32)
            self.then_y[...] = total.astype(BF)
            for d in (1, 3, 2):
                links.start(self.then_y.at[(y + d) % 4], self.got_y.at[d - 1], self.y + d, step_y(d))

        def third(self):
            for d in (1, 3, 2):
                links.arrived(self.got_x.at[d - 1], self.x + d, step_x(4 - d))
            total = self.then_x[:, x].astype(F32)
            for d in (1, 2, 3):
                total = total + self.got_x[d - 1].astype(F32)
            self.zs[:, :, left] = total
            for d in (1, 3, 2):
                links.arrived(self.got_y.at[d - 1], self.y + d, step_y(4 - d))
            total = self.then_y[y].astype(F32)
            for d in (1, 2, 3):
                total = total + self.got_y[d - 1].astype(F32)
            self.zs[:, :, right] = total
            links.start(self.zs.at[1 - zh, rows_mine], self.fr.at[1], self.z + 1, away)
            links.start(self.zs.at[1 - zh, rows_other], self.fr.at[2], self.z + 2, across)
            links.start(self.zs.at[zh, rows_other], self.fr.at[0], self.z, core)

        def last(self, ref, scale):
            links.arrived(self.fr.at[0], self.z, core)
            links.arrived(self.fr.at[1], self.z + 1, away)
            links.arrived(self.fr.at[2], self.z + 2, across)
            ref[:, mine] = ((self.zs[zh, rows_mine, :] + self.fr[1]) * scale).astype(BF)
            ref[:, other] = ((self.fr[0] + self.fr[2]) * scale).astype(BF)

        def finish(self):
            for d in (1, 2, 3):
                src = self.core_in.at[0, :, :, :, left]
                links.copy(src, self.ring_y.at[0], self.yx + d, step_y(d)).wait_send()

    left, right = pl.ds(0, 512), pl.ds(512, 512)
    rows_other = pl.ds(pl.multiple_of((1 - c) * 8, 8), 8)
    rows_mine = pl.ds(pl.multiple_of(c * 8, 8), 8)
    steps = (t, (t + 2) % 4, partner[0], (partner[0] + 2) % 4)
    blocks = (yt, yf, yp, ypf)
    out_sum = Spread(*o_refs)
    in_sum = Spread(*i_refs)

    for n in (0, 1):
        out_sum.block(n, hb[blocks[n]], down_w[...])
    links.arrived(hb.at[yp], h2, partner)
    out_sum.block(2, hb[yp], down_w[...])
    links.arrived(hb.at[ypf], h3, partner)
    out_sum.block(3, hb[ypf], down_w[...])
    for n in range(4):
        out_sum.first(n)

    def pass_on():
        for u in (0, 1):
            links.arrived(db.at[yf, units[u]], g1 + u, far)
            links.start(db.at[yf, units[u]], db.at[yf, units[u]], g3 + u, partner)

    hq_all = jnp.concatenate([hb[n] for n in range(4)], axis=1)

    def down_tile(i, top):
        columns = pl.ds(pl.multiple_of(i * 256, 256), 256)
        rows = gb[:, :, :, :, columns].reshape(512, 256)
        value = jnp.dot(hq_all, rows, preferred_element_type=F32) * (s1 * s2)
        down_g[:, columns] = value.astype(BF)
        return jnp.maximum(top, jnp.max(jnp.abs(value)))

    max_d = lax.fori_loop(0, 4, down_tile, jnp.float32(0.0))
    pass_on()
    in_sum.block(0, db[yt], wide_w[...])
    in_sum.block(1, db[yf], wide_w[...])
    out_sum.second()
    max_d = lax.fori_loop(4, 8, down_tile, max_d)
    store_d = pltpu.make_async_copy(down_g, wdown_hbm, store_sem.at[0])
    store_d.start()
    in_sum.first(0)
    in_sum.first(1)
    for u in (0, 1):
        links.arrived(db.at[yp, units[u]], g2 + u, partner)
    in_sum.block(2, db[yp], wide_w[...])
    out_sum.third()
    for u in (0, 1):
        links.arrived(db.at[ypf, units[u]], g3 + u, partner)
    in_sum.block(3, db[ypf], wide_w[...])

    dq_all = jnp.concatenate([db[n] for n in range(4)], axis=1)

    def wide_tile(i, top):
        columns = pl.ds(pl.multiple_of(i * 256, 256), 256)
        rows = xb[:, :, :, :, columns].reshape(512, 256)
        value = jnp.dot(dq_all, rows, preferred_element_type=F32) * (s0 * s3)
        wide_g[:, columns] = value.astype(BF)
        return jnp.maximum(top, jnp.max(jnp.abs(value)))

    in_sum.first(2)
    max_w = lax.fori_loop(0, 3, wide_tile, jnp.float32(0.0))
    in_sum.first(3)
    max_w = lax.fori_loop(3, 8, wide_tile, max_w)
    store_w = pltpu.make_async_copy(wide_g, wide_hbm, store_sem.at[1])
    store_w.start()

    row = lax.broadcasted_iota(jnp.int32, (8, 128), 0)
    tops = jnp.zeros((8, 128), F32)
    for n, value in enumerate((max_x, max_h, max_g, max_p, max_w, max_d)):
        tops = jnp.where(row == n, value, tops)

    def send_tops(stage, value, offsets):
        first = links.slots(len(offsets))
        max_s[stage] = value
        for n, offset in enumerate(offsets):
            links.start(max_s.at[stage], max_r.at[stage, n], first + n, device(**offset))
        return first

    def take_tops(stage, value, offsets, first):
        for n, offset in enumerate(offsets):
            back = {name: -d for name, d in offset.items()}
            links.arrived(max_r.at[stage, n], first + n, device(**back))
            value = jnp.maximum(value, max_r[stage, n])
        return value

    plane = [dict(dx=d, dc=e) for d in range(4) for e in range(2) if d or e]
    depth = [dict(dt=d, dz=e) for d in range(4) for e in range(2) if d or e]
    column = [dict(dy=d) for d in (1, 2, 3)]
    first = send_tops(0, tops, plane)
    in_sum.second()
    tops = take_tops(0, tops, plane, first)
    first = send_tops(1, tops, column)
    in_sum.third()
    tops = take_tops(1, tops, column, first)
    first = send_tops(2, tops, depth)
    out_sum.last(out_ref, s1)
    tops = take_tops(2, tops, depth, first)
    peaks_ref[pl.ds(0, 8), :] = tops
    peaks_ref[pl.ds(8, 8), :] = jnp.log(tops + 1e-6)
    in_sum.last(in_grad_ref, s3)

    out_sum.finish()
    in_sum.finish()
    links.finish()
    store_d.wait()
    store_w.wait()
    assert links.used <= N_SEMS


def scale_grads(
    peaks, out_in, in_grad_in, wide_hbm, wdown_hbm,
    gate_out, up_out, down_out, out_ref, in_grad_ref, amaxes_ref,
    held, scaled, load_sem, store_sem,
):
    size = UNITS // 2
    halves = [pl.ds(n * size, size) for n in range(4)]
    sources = [wide_hbm.at[rows] for rows in halves] + [wdown_hbm.at[rows] for rows in halves[:2]]
    targets = [ref.at[rows] for ref in (gate_out, up_out, down_out) for rows in halves[:2]]
    loads = [
        pltpu.make_async_copy(source, held.at[n], load_sem.at[n]) for n, source in enumerate(sources)
    ]
    stores = [
        pltpu.make_async_copy(scaled.at[n], target, store_sem.at[n])
        for n, target in enumerate(targets)
    ]
    for load in loads:
        load.start()
    for n in range(6):
        amaxes_ref[n] = peaks[8 + n, 0]
    out_ref[...] = out_in[...]
    in_grad_ref[...] = in_grad_in[...]
    over_wide = 1.0 / (peaks[4, 0] + 1e-6)
    over_down = 1.0 / (peaks[5, 0] + 1e-6)
    for n in range(6):
        loads[n].wait()
        over = over_wide if n < 4 else over_down
        scaled[n] = (held[n].astype(F32) * over).astype(BF)
        stores[n].start()
    for store in stores:
        store.wait()


def shards(tokens, gate_weight, up_weight, down_weight, out_grad, amax_prior):
    vmem = pl.BlockSpec(memory_space=pltpu.VMEM)
    hbm = pl.BlockSpec(memory_space=pl.ANY)
    V = pltpu.VMEM
    sum_scratch = (
        V((4, 2, 4, 16, 2048), BF), V((4, 2, 4, 16, HALF), BF),
        V((3, 2, 4, 16, 512), BF), V((3, 4, 2, 16, 512), BF),
        V((2, 4, 16, 512), BF), V((4, 2, 16, 512), BF),
        V((3, 2, 16, 512), BF), V((3, 2, 16, 512), BF),
        V((2, 16, HALF), F32), V((3, 8, HALF), F32),
    )
    output, input_grad, wide, wdown, peaks = pl.pallas_call(
        kernel,
        out_shape=(
            jax.ShapeDtypeStruct((8, 2048), BF),
            jax.ShapeDtypeStruct((8, 2048), BF),
            jax.ShapeDtypeStruct((WIDE, 2048), BF),
            jax.ShapeDtypeStruct((UNITS, 2048), BF),
            jax.ShapeDtypeStruct((16, 128), F32),
        ),
        in_specs=[pl.BlockSpec(memory_space=pltpu.SMEM), vmem, vmem, hbm, hbm, hbm],
        out_specs=(vmem, vmem, hbm, hbm, vmem),
        scratch_shapes=[
            V((4, 2, 4, 16, 2048), BF), V((4, 2, 4, 16, 2048), BF),
            V((WIDE, 2048), BF), V((UNITS, 2048), BF),
            V((16, 2048), BF), V((3, 16, HALF), BF),
            V((2, 2, UNITS, 128), BF), V((2, 2, UNITS, 128), F32), V((2, 2, UNITS, 128), BF),
            V((2, UNITS, 128), BF), V((2, UNITS, 128), BF),
            V((2, UNITS, 128), BF), V((2, UNITS, 128), F32), V((2, UNITS, 128), BF),
            V((UNITS, 128), BF), V((UNITS, 128), BF),
            V((4, UNITS, 128), BF), V((4, WIDE, 128), BF),
            sum_scratch, sum_scratch,
            V((WIDE, 2048), BF), V((UNITS, 2048), BF),
            V((3, 8, 128), F32), V((3, 7, 8, 128), F32),
            pltpu.SemaphoreType.DMA((N_SEMS,)), pltpu.SemaphoreType.DMA((N_SEMS,)),
            pltpu.SemaphoreType.DMA((3,)), pltpu.SemaphoreType.DMA((2,)),
        ],
        compiler_params=pltpu.CompilerParams(
            collective_id=0, has_side_effects=True, vmem_limit_bytes=60 << 20
        ),
        name="layer",
    )(amax_prior, tokens, out_grad, gate_weight.T, up_weight.T, down_weight)
    full = (
        jax.ShapeDtypeStruct((UNITS, 2048), BF),
        jax.ShapeDtypeStruct((UNITS, 2048), BF),
        jax.ShapeDtypeStruct((UNITS, 2048), BF),
        jax.ShapeDtypeStruct((8, 2048), BF),
        jax.ShapeDtypeStruct((8, 2048), BF),
        jax.ShapeDtypeStruct((6,), F32),
    )
    smem = pl.BlockSpec(memory_space=pltpu.SMEM)
    gate_grad, up_grad, down_grad, output, input_grad, amaxes = pl.pallas_call(
        scale_grads,
        out_shape=full,
        in_specs=[smem, vmem, vmem, hbm, hbm],
        out_specs=(hbm, hbm, hbm, vmem, vmem, smem),
        scratch_shapes=[
            V((6, UNITS // 2, 2048), BF),
            V((6, UNITS // 2, 2048), BF),
            pltpu.SemaphoreType.DMA((6,)),
            pltpu.SemaphoreType.DMA((6,)),
        ],
        compiler_params=pltpu.CompilerParams(vmem_limit_bytes=60 << 20),
        name="scale",
    )(peaks, output, input_grad, wide, wdown)
    return (output, input_grad, gate_grad.T, up_grad.T, down_grad, amaxes)


def solution(mesh):
    placed = (
        P("hid", "tok"),
        P("tok", "hid"),
        P("tok", "hid"),
        P("hid", "tok"),
        P("hid", "tok"),
        P(),
    )
    return jax.shard_map(
        shards,
        mesh=mesh,
        in_specs=placed,
        out_specs=(
            P("hid", "tok"),
            P("hid", "tok"),
            P("tok", "hid"),
            P("tok", "hid"),
            P("hid", "tok"),
            P(),
        ),
        check_vma=False,
    )
```

```python
import jax
import jax.numpy as jnp
from jax import lax
from jax.experimental import pallas as pl
from jax.experimental.pallas import tpu as pltpu
from jax.sharding import PartitionSpec as P

MESH = pl.DeviceIdType.MESH
BF = jnp.bfloat16
F32 = jnp.float32
HALF = 1024
UNITS = 416
WIDE = 832


def contract_last(left, right):
    return lax.dot_general(left, right, (((1,), (1,)), ((), ())), preferred_element_type=F32)


def contract_first(left, right):
    return lax.dot_general(left, right, (((0,), (0,)), ((), ())), preferred_element_type=F32)


def quantize(value, scale):
    return jnp.clip(value / scale, -448.0, 448.0).astype(BF)


class Links:
    def __init__(self, send, recv):
        self.send, self.recv, self.used, self.open = send, recv, 0, []

    def slots(self, count):
        first = self.used
        self.used += count
        return first

    def copy(self, src, dst, slot, device):
        return pltpu.make_async_remote_copy(
            src_ref=src,
            dst_ref=dst,
            send_sem=self.send.at[slot],
            recv_sem=self.recv.at[slot],
            device_id=device,
            device_id_type=MESH,
        )

    def start(self, src, dst, slot, device):
        copy = self.copy(src, dst, slot, device)
        copy.start()
        self.open.append(copy)

    def arrived(self, dst, slot, device):
        self.copy(dst, dst, slot, device).wait_recv()

    def finish(self):
        for copy in self.open:
            copy.wait_send()


N_SEMS = 260


def kernel(
    prior, tokens, out_grad, gate_hbm, up_hbm, down_hbm,
    out_ref, in_grad_ref, wide_hbm, wdown_hbm, peaks_ref,
    xb, gb, wide_w, down_w, swap_out, swap_in,
    part, keep, got1, send2, got2,
    dpart, dkeep, dgot1, dsend2, dgot2,
    hb, db,
    o_refs, i_refs,
    wide_g, down_g, max_s, max_r,
    send_sem, recv_sem, load_sem, store_sem,
):
    t = lax.axis_index("tok")
    h = lax.axis_index("hid")
    y, zh, x, c = h // 16, (h // 8) % 2, (h // 2) % 4, h % 2
    p, s = t % 2, t // 2

    def device(dt=0, dy=0, dz=0, dx=0, dc=0):
        hid = ((((y + dy) % 4) * 2 + (zh + dz) % 2) * 4 + (x + dx) % 4) * 2 + (c + dc) % 2
        return ((t + dt) % 4, hid)

    def beside():
        return (t + 1 - 2 * p, h)

    peers = [device(dx=d, dc=e) for d in range(4) for e in range(2) if d or e]
    peers += [device(dy=d) for d in (1, 2, 3)]
    peers += [device(dt=d, dz=e) for d in range(4) for e in range(2) if d or e]
    peers += [device(dz=1, dc=1)]
    barrier = pltpu.get_barrier_semaphore()
    for peer in peers:
        pl.semaphore_signal(barrier, inc=1, device_id=peer, device_id_type=MESH)

    loads = [
        pltpu.make_async_copy(gate_hbm, wide_w.at[pl.ds(0, UNITS)], load_sem.at[0]),
        pltpu.make_async_copy(up_hbm, wide_w.at[pl.ds(UNITS, UNITS)], load_sem.at[1]),
        pltpu.make_async_copy(down_hbm, down_w, load_sem.at[2]),
    ]
    for load in loads:
        load.start()

    s0, s1, s2, s3 = [prior[i] / 448.0 for i in range(4)]
    mine = pl.ds(pl.multiple_of(c * HALF, HALF), HALF)
    other = pl.ds(pl.multiple_of((1 - c) * HALF, HALF), HALF)

    tok_f = tokens[...].astype(F32)
    og_f = out_grad[...].astype(F32)
    max_x = jnp.max(jnp.abs(tok_f))
    max_g = jnp.max(jnp.abs(og_f))
    swap_out[...] = jnp.concatenate(
        [quantize(tok_f, s0).astype(F32), quantize(og_f, s2).astype(F32)], axis=0
    ).astype(BF)

    links = Links(send_sem, recv_sem)
    core = device(dc=1)

    pl.semaphore_wait(barrier, len(peers))

    first = links.slots(3)
    away = device(dz=1)
    across = device(dz=1, dc=1)
    links.start(swap_out.at[:, mine], swap_in.at[1], first + 1, away)
    links.start(swap_out.at[:, other], swap_in.at[2], first + 2, across)
    links.start(swap_out.at[:, other], swap_in.at[0], first, core)

    def place(z, own, theirs):
        own, theirs = own.astype(F32), theirs.astype(F32)
        low = jnp.where(c == 0, own, theirs)
        high = jnp.where(c == 0, theirs, own)
        xb[y, z, x, :, mine] = jnp.concatenate([low[0:8], high[0:8]], axis=0).astype(BF)
        gb[y, z, x, :, mine] = jnp.concatenate([low[8:16], high[8:16]], axis=0).astype(BF)

    links.arrived(swap_in.at[0], first, core)
    place(zh, swap_out[:, mine], swap_in[0])
    def step_x(d):
        return device(dx=d)

    def step_y(d):
        return device(dy=d)

    cols_xy = pl.ds(pl.multiple_of(c * HALF, 512), 512)
    cols_yx = pl.ds(pl.multiple_of(c * HALF + 512, 512), 512)

    class Gather:
        def __init__(self, buf):
            self.buf = buf
            self.first = {a: (links.slots(4), links.slots(4)) for a in (0, 1)}
            self.second = {a: (links.slots(4), links.slots(4)) for a in (0, 1)}
            self.swap = {a: (links.slots(4), links.slots(4)) for a in (0, 1)}

        def level(self, a):
            return zh if a == 0 else 1 - zh

        def send_first(self, a):
            z = self.level(a)
            for d in (1, 3, 2):
                block = self.buf.at[y, z, x, :, cols_xy]
                links.start(block, block, self.first[a][0] + d, step_x(d))
                block = self.buf.at[y, z, x, :, cols_yx]
                links.start(block, block, self.first[a][1] + d, step_y(d))

        def wait_first(self, a):
            z = self.level(a)
            for d in (1, 3, 2):
                block = self.buf.at[y, z, (x - d) % 4, :, cols_xy]
                links.arrived(block, self.first[a][0] + d, step_x(4 - d))
                block = self.buf.at[(y - d) % 4, z, x, :, cols_yx]
                links.arrived(block, self.first[a][1] + d, step_y(4 - d))

        def send_second(self, a):
            z = self.level(a)
            for d in (1, 3, 2):
                rows = self.buf.at[y, z, :, :, cols_xy]
                links.start(rows, rows, self.second[a][0] + d, step_y(d))
                rows = self.buf.at[:, z, x, :, cols_yx]
                links.start(rows, rows, self.second[a][1] + d, step_x(d))

        def wait_second(self, a, d):
            z = self.level(a)
            rows = self.buf.at[(y - d) % 4, z, :, :, cols_xy]
            links.arrived(rows, self.second[a][0] + d, step_y(4 - d))
            rows = self.buf.at[:, z, (x - d) % 4, :, cols_yx]
            links.arrived(rows, self.second[a][1] + d, step_x(4 - d))

        def send_swap(self, a, d):
            z = self.level(a)
            rows = self.buf.at[(y - d) % 4, z, :, :, cols_xy]
            links.start(rows, rows, self.swap[a][0] + d, core)
            rows = self.buf.at[:, z, (x - d) % 4, :, cols_yx]
            links.start(rows, rows, self.swap[a][1] + d, core)

        def wait_swap(self, a):
            z = self.level(a)
            there_xy = pl.ds(pl.multiple_of((1 - c) * HALF, 512), 512)
            there_yx = pl.ds(pl.multiple_of((1 - c) * HALF + 512, 512), 512)
            for d in (0, 1, 3, 2):
                rows = self.buf.at[(y - d) % 4, z, :, :, there_xy]
                links.arrived(rows, self.swap[a][0] + d, core)
                rows = self.buf.at[:, z, (x - d) % 4, :, there_yx]
                links.arrived(rows, self.swap[a][1] + d, core)

        def complete(self, a):
            for d in (1, 3, 2):
                self.wait_second(a, d)
                self.send_swap(a, d)
            self.wait_swap(a)

    gx, gg = Gather(xb), Gather(gb)
    gx.send_first(0)
    gg.send_first(0)
    gx.wait_first(0)
    gx.send_second(0)
    links.arrived(swap_in.at[1], first + 1, away)
    links.arrived(swap_in.at[2], first + 2, across)
    place(1 - zh, swap_in[1], swap_in[2])
    gx.send_first(1)
    gg.send_first(1)
    gx.send_swap(0, 0)
    gg.wait_first(0)
    gg.send_second(0)
    gx.wait_first(1)
    gx.send_second(1)
    gg.wait_first(1)
    gg.send_second(1)
    gx.send_swap(1, 0)
    gg.send_swap(0, 0)
    gg.send_swap(1, 0)
    for load in loads:
        load.wait()
    gx.complete(0)

    order = ((1 - p) + 2 * (1 - s), (1 - p) + 2 * s, p + 2 * (1 - s), p + 2 * s)
    r1, r2 = links.slots(4), links.slots(2)
    d1, d2 = links.slots(2), links.slots(1)
    partner = beside()
    far = device(dt=2)
    units = (pl.ds(0, UNITS), pl.ds(UNITS, UNITS))
    lower = lax.broadcasted_iota(jnp.int32, (UNITS, 128), 1) < 64

    def turn(value):
        return pltpu.roll(value, 64, 1)

    def pair(buf, j, z=None):
        two = [buf[(y + k) % 4] if z is None else buf[(y + k) % 4, z] for k in order[j : j + 2]]
        return jnp.concatenate([value.reshape(-1, 2048) for value in two], axis=0)

    def gate_and_up(j, z):
        value = contract_last(wide_w[...], pair(xb, j, z))
        gate, up = value[:UNITS], value[UNITS:]
        return jnp.where(lower, gate, turn(up)), jnp.where(lower, turn(gate), up)

    for a, z in ((0, zh), (1, 1 - zh)):
        if a:
            gx.complete(1)
        for j, to, value in zip((0, 1), (1 - s, s), gate_and_up(0, z)):
            part[j, a] = value.astype(BF)
            links.start(part.at[j, a], got1.at[to, z], r1 + 2 * to + a, partner)
        for j, value in zip((0, 1), gate_and_up(2, z)):
            keep[j, z] = value

    def send_far(a, z):
        links.arrived(got1.at[1 - s, z], r1 + 2 * (1 - s) + a, partner)
        send2[z] = (keep[0, z] + got1[1 - s, z].astype(F32)).astype(BF)
        links.start(send2.at[z], got2.at[z], r2 + a, far)

    send_far(0, zh)
    gg.complete(0)
    gg.complete(1)
    value = contract_last(down_w[...], pair(gb, 0))
    dpart[0] = value[:, :128].astype(BF)
    dpart[1] = value[:, 128:].astype(BF)
    links.start(dpart.at[0], dgot1.at[1 - s], d1 + (1 - s), partner)
    value = contract_last(down_w[...], pair(gb, 2))
    dkeep[0] = value[:, :128]
    dkeep[1] = value[:, 128:]
    send_far(1, 1 - zh)
    links.arrived(dgot1.at[1 - s], d1 + (1 - s), partner)
    dsend2[...] = (dkeep[0] + dgot1[1 - s].astype(F32)).astype(BF)
    links.start(dsend2, dgot2, d2, far)
    links.start(dpart.at[1], dgot1.at[s], d1 + s, partner)
    yt = (y + t) % 4
    h1, h2, h3 = links.slots(1), links.slots(1), links.slots(1)
    g1, g2, g3 = links.slots(2), links.slots(2), links.slots(2)

    for a, z in ((0, zh), (1, 1 - zh)):
        links.arrived(got1.at[s, z], r1 + 2 * s + a, partner)
        links.arrived(got2.at[z], r2 + a, far)
    low, high = [
        (keep[1, z] + got1[s, z].astype(F32) + got2[z].astype(F32)) * s0 for z in (0, 1)
    ]
    gate = jnp.where(lower, low, turn(high))
    up = jnp.where(lower, turn(low), high)
    sig = jax.nn.sigmoid(gate)
    act = gate * sig
    hidden = act * up
    max_h = jnp.max(jnp.abs(hidden))
    hb[yt] = quantize(hidden, s1)
    links.start(hb.at[yt], hb.at[yt], h1, far)
    links.start(hb.at[yt], hb.at[yt], h2, partner)

    links.arrived(dgot1.at[s], d1 + s, partner)
    links.arrived(dgot2, d2, far)
    dhidden = (dkeep[1] + dgot1[s].astype(F32) + dgot2[...].astype(F32)) * s2
    dgate = dhidden * up * sig * (1.0 + gate * (1.0 - sig))
    dup = dhidden * act
    max_p = jnp.maximum(jnp.max(jnp.abs(dgate)), jnp.max(jnp.abs(dup)))
    for u, value in ((0, dgate), (1, dup)):
        db[yt, units[u]] = quantize(value, s3)
        links.start(db.at[yt, units[u]], db.at[yt, units[u]], g1 + u, far)
    for u in (0, 1):
        links.start(db.at[yt, units[u]], db.at[yt, units[u]], g2 + u, partner)
    yf = (y + (t + 2) % 4) % 4
    yp = (y + partner[0]) % 4
    ypf = (y + (partner[0] + 2) % 4) % 4
    links.arrived(hb.at[yf], h1, far)
    links.start(hb.at[yf], hb.at[yf], h3, partner)

    class Spread:
        def __init__(self, part, core_in, ring_y, ring_x, then_x, then_y, got_x, got_y, zs, fr):
            self.part, self.core_in, self.ring_y, self.ring_x = part, core_in, ring_y, ring_x
            self.then_x, self.then_y, self.got_x, self.got_y = then_x, then_y, got_x, got_y
            self.zs, self.fr = zs, fr
            self.cores, self.yx, self.xy = links.slots(4), links.slots(4), links.slots(16)
            self.x, self.y, self.z = links.slots(4), links.slots(4), links.slots(3)

        def block(self, n, left, right):
            value = contract_first(left, right)
            at = blocks[n]
            self.part[at] = value.astype(BF).reshape(2, 4, 16, 2048)
            links.start(self.part.at[at, :, :, :, other], self.core_in.at[at], self.cores + n, core)

        def first(self, n):
            at, d = blocks[n], steps[n]
            links.arrived(self.core_in.at[at], self.cores + n, core)
            value = self.part[at, :, :, :, mine].astype(F32) + self.core_in[at].astype(F32)
            self.core_in[at] = value.astype(BF)

            @pl.when(d != 0)
            def _():
                src = self.core_in.at[at, :, :, :, left]
                links.copy(src, self.ring_y.at[d - 1], self.yx + d, device(dy=d)).start()

            for e in (1, 3, 2):
                src = self.core_in.at[at, :, (x + e) % 4, :, right]
                links.start(src, self.ring_x.at[e - 1, at], self.xy + 4 * n + e, step_x(e))

        def second(self):
            for d in (1, 3, 2):
                links.arrived(self.ring_y.at[d - 1], self.yx + d, step_y(4 - d))
            total = self.core_in[y, :, :, :, left].astype(F32)
            for d in (1, 2, 3):
                total = total + self.ring_y[d - 1].astype(F32)
            self.then_x[...] = total.astype(BF)
            for d in (1, 3, 2):
                links.start(self.then_x.at[:, (x + d) % 4], self.got_x.at[d - 1], self.x + d, step_x(d))
            for n in range(4):
                for e in (1, 3, 2):
                    links.arrived(self.ring_x.at[e - 1, blocks[n]], self.xy + 4 * n + e, step_x(4 - e))
            total = self.core_in[:, :, x, :, right].astype(F32)
            for d in (1, 2, 3):
                total = total + self.ring_x[d - 1].astype(F32)
            self.then_y[...] = total.astype(BF)
            for d in (1, 3, 2):
                links.start(self.then_y.at[(y + d) % 4], self.got_y.at[d - 1], self.y + d, step_y(d))

        def third(self):
            for d in (1, 3, 2):
                links.arrived(self.got_x.at[d - 1], self.x + d, step_x(4 - d))
            total = self.then_x[:, x].astype(F32)
            for d in (1, 2, 3):
                total = total + self.got_x[d - 1].astype(F32)
            self.zs[:, :, left] = total
            for d in (1, 3, 2):
                links.arrived(self.got_y.at[d - 1], self.y + d, step_y(4 - d))
            total = self.then_y[y].astype(F32)
            for d in (1, 2, 3):
                total = total + self.got_y[d - 1].astype(F32)
            self.zs[:, :, right] = total
            links.start(self.zs.at[1 - zh, rows_mine], self.fr.at[1], self.z + 1, away)
            links.start(self.zs.at[1 - zh, rows_other], self.fr.at[2], self.z + 2, across)
            links.start(self.zs.at[zh, rows_other], self.fr.at[0], self.z, core)

        def last(self, ref, scale):
            links.arrived(self.fr.at[0], self.z, core)
            links.arrived(self.fr.at[1], self.z + 1, away)
            links.arrived(self.fr.at[2], self.z + 2, across)
            ref[:, mine] = ((self.zs[zh, rows_mine, :] + self.fr[1]) * scale).astype(BF)
            ref[:, other] = ((self.fr[0] + self.fr[2]) * scale).astype(BF)

        def finish(self):
            for d in (1, 2, 3):
                src = self.core_in.at[0, :, :, :, left]
                links.copy(src, self.ring_y.at[0], self.yx + d, step_y(d)).wait_send()

    left, right = pl.ds(0, 512), pl.ds(512, 512)
    rows_other = pl.ds(pl.multiple_of((1 - c) * 8, 8), 8)
    rows_mine = pl.ds(pl.multiple_of(c * 8, 8), 8)
    steps = (t, (t + 2) % 4, partner[0], (partner[0] + 2) % 4)
    blocks = (yt, yf, yp, ypf)
    out_sum = Spread(*o_refs)
    in_sum = Spread(*i_refs)

    def pass_on():
        for u in (0, 1):
            links.arrived(db.at[yf, units[u]], g1 + u, far)
            links.start(db.at[yf, units[u]], db.at[yf, units[u]], g3 + u, partner)

    out_sum.block(0, hb[yt], down_w[...])
    out_sum.block(1, hb[yf], down_w[...])
    links.arrived(hb.at[yp], h2, partner)
    out_sum.block(2, hb[yp], down_w[...])
    in_sum.block(0, db[yt], wide_w[...])
    for n in range(3):
        out_sum.first(n)
    in_sum.first(0)
    pass_on()
    in_sum.block(1, db[yf], wide_w[...])
    links.arrived(hb.at[ypf], h3, partner)
    out_sum.block(3, hb[ypf], down_w[...])
    in_sum.first(1)

    hq_all = jnp.concatenate([hb[n] for n in range(4)], axis=1)

    def down_tile(i, top):
        columns = pl.ds(pl.multiple_of(i * 256, 256), 256)
        rows = gb[:, :, :, :, columns].reshape(512, 256)
        value = jnp.dot(hq_all, rows, preferred_element_type=F32) * (s1 * s2)
        down_g[:, columns] = value.astype(BF)
        return jnp.maximum(top, jnp.max(jnp.abs(value)))

    max_d = lax.fori_loop(0, 4, down_tile, jnp.float32(0.0))
    out_sum.first(3)
    for u in (0, 1):
        links.arrived(db.at[yp, units[u]], g2 + u, partner)
    in_sum.block(2, db[yp], wide_w[...])
    max_d = lax.fori_loop(4, 8, down_tile, max_d)
    store_d = pltpu.make_async_copy(down_g, wdown_hbm, store_sem.at[0])
    store_d.start()
    in_sum.first(2)
    for u in (0, 1):
        links.arrived(db.at[ypf, units[u]], g3 + u, partner)
    in_sum.block(3, db[ypf], wide_w[...])

    dq_all = jnp.concatenate([db[n] for n in range(4)], axis=1)

    def wide_tile(i, top):
        columns = pl.ds(pl.multiple_of(i * 256, 256), 256)
        rows = xb[:, :, :, :, columns].reshape(512, 256)
        value = jnp.dot(dq_all, rows, preferred_element_type=F32) * (s0 * s3)
        wide_g[:, columns] = value.astype(BF)
        return jnp.maximum(top, jnp.max(jnp.abs(value)))

    max_w = lax.fori_loop(0, 4, wide_tile, jnp.float32(0.0))
    in_sum.first(3)
    max_w = lax.fori_loop(4, 8, wide_tile, max_w)
    store_w = pltpu.make_async_copy(wide_g, wide_hbm, store_sem.at[1])
    store_w.start()

    row = lax.broadcasted_iota(jnp.int32, (8, 128), 0)
    tops = jnp.zeros((8, 128), F32)
    for n, value in enumerate((max_x, max_h, max_g, max_p, max_w, max_d)):
        tops = jnp.where(row == n, value, tops)

    def send_tops(stage, value, offsets):
        first = links.slots(len(offsets))
        max_s[stage] = value
        for n, offset in enumerate(offsets):
            links.start(max_s.at[stage], max_r.at[stage, n], first + n, device(**offset))
        return first

    def take_tops(stage, value, offsets, first):
        for n, offset in enumerate(offsets):
            back = {name: -d for name, d in offset.items()}
            links.arrived(max_r.at[stage, n], first + n, device(**back))
            value = jnp.maximum(value, max_r[stage, n])
        return value

    plane = [dict(dx=d, dc=e) for d in range(4) for e in range(2) if d or e]
    depth = [dict(dt=d, dz=e) for d in range(4) for e in range(2) if d or e]
    column = [dict(dy=d) for d in (1, 2, 3)]
    first = send_tops(0, tops, plane)
    out_sum.second()
    in_sum.second()
    tops = take_tops(0, tops, plane, first)
    first = send_tops(1, tops, column)
    out_sum.third()
    in_sum.third()
    tops = take_tops(1, tops, column, first)
    first = send_tops(2, tops, depth)
    out_sum.last(out_ref, s1)
    tops = take_tops(2, tops, depth, first)
    peaks_ref[pl.ds(0, 8), :] = tops
    peaks_ref[pl.ds(8, 8), :] = jnp.log(tops + 1e-6)
    in_sum.last(in_grad_ref, s3)

    out_sum.finish()
    in_sum.finish()
    links.finish()
    store_d.wait()
    store_w.wait()
    assert links.used <= N_SEMS


def scale_grads(
    peaks, out_in, in_grad_in, wide_hbm, wdown_hbm,
    gate_out, up_out, down_out, out_ref, in_grad_ref, amaxes_ref,
    held, scaled, load_sem, store_sem,
):
    sources = [wide_hbm.at[pl.ds(0, UNITS)], wide_hbm.at[pl.ds(UNITS, UNITS)], wdown_hbm]
    targets = [gate_out, up_out, down_out]
    loads = [
        pltpu.make_async_copy(source, held.at[n], load_sem.at[n]) for n, source in enumerate(sources)
    ]
    stores = [
        pltpu.make_async_copy(scaled.at[n], target, store_sem.at[n])
        for n, target in enumerate(targets)
    ]
    for load in loads:
        load.start()
    for n in range(6):
        amaxes_ref[n] = peaks[8 + n, 0]
    out_ref[...] = out_in[...]
    in_grad_ref[...] = in_grad_in[...]
    over_wide = 1.0 / (peaks[4, 0] + 1e-6)
    over_down = 1.0 / (peaks[5, 0] + 1e-6)
    for n in range(3):
        loads[n].wait()
        over = over_wide if n < 2 else over_down
        scaled[n] = (held[n].astype(F32) * over).astype(BF)
        stores[n].start()
    for store in stores:
        store.wait()


def shards(tokens, gate_weight, up_weight, down_weight, out_grad, amax_prior):
    vmem = pl.BlockSpec(memory_space=pltpu.VMEM)
    hbm = pl.BlockSpec(memory_space=pl.ANY)
    V = pltpu.VMEM
    sum_scratch = (
        V((4, 2, 4, 16, 2048), BF), V((4, 2, 4, 16, HALF), BF),
        V((3, 2, 4, 16, 512), BF), V((3, 4, 2, 16, 512), BF),
        V((2, 4, 16, 512), BF), V((4, 2, 16, 512), BF),
        V((3, 2, 16, 512), BF), V((3, 2, 16, 512), BF),
        V((2, 16, HALF), F32), V((3, 8, HALF), F32),
    )
    output, input_grad, wide, wdown, peaks = pl.pallas_call(
        kernel,
        out_shape=(
            jax.ShapeDtypeStruct((8, 2048), BF),
            jax.ShapeDtypeStruct((8, 2048), BF),
            jax.ShapeDtypeStruct((WIDE, 2048), BF),
            jax.ShapeDtypeStruct((UNITS, 2048), BF),
            jax.ShapeDtypeStruct((16, 128), F32),
        ),
        in_specs=[pl.BlockSpec(memory_space=pltpu.SMEM), vmem, vmem, hbm, hbm, hbm],
        out_specs=(vmem, vmem, hbm, hbm, vmem),
        scratch_shapes=[
            V((4, 2, 4, 16, 2048), BF), V((4, 2, 4, 16, 2048), BF),
            V((WIDE, 2048), BF), V((UNITS, 2048), BF),
            V((16, 2048), BF), V((3, 16, HALF), BF),
            V((2, 2, UNITS, 128), BF), V((2, 2, UNITS, 128), F32), V((2, 2, UNITS, 128), BF),
            V((2, UNITS, 128), BF), V((2, UNITS, 128), BF),
            V((2, UNITS, 128), BF), V((2, UNITS, 128), F32), V((2, UNITS, 128), BF),
            V((UNITS, 128), BF), V((UNITS, 128), BF),
            V((4, UNITS, 128), BF), V((4, WIDE, 128), BF),
            sum_scratch, sum_scratch,
            V((WIDE, 2048), BF), V((UNITS, 2048), BF),
            V((3, 8, 128), F32), V((3, 7, 8, 128), F32),
            pltpu.SemaphoreType.DMA((N_SEMS,)), pltpu.SemaphoreType.DMA((N_SEMS,)),
            pltpu.SemaphoreType.DMA((3,)), pltpu.SemaphoreType.DMA((2,)),
        ],
        compiler_params=pltpu.CompilerParams(
            collective_id=0, has_side_effects=True, vmem_limit_bytes=60 << 20
        ),
        name="layer",
    )(amax_prior, tokens, out_grad, gate_weight.T, up_weight.T, down_weight)
    full = (
        jax.ShapeDtypeStruct((UNITS, 2048), BF),
        jax.ShapeDtypeStruct((UNITS, 2048), BF),
        jax.ShapeDtypeStruct((UNITS, 2048), BF),
        jax.ShapeDtypeStruct((8, 2048), BF),
        jax.ShapeDtypeStruct((8, 2048), BF),
        jax.ShapeDtypeStruct((6,), F32),
    )
    smem = pl.BlockSpec(memory_space=pltpu.SMEM)
    gate_grad, up_grad, down_grad, output, input_grad, amaxes = pl.pallas_call(
        scale_grads,
        out_shape=full,
        in_specs=[smem, vmem, vmem, hbm, hbm],
        out_specs=(hbm, hbm, hbm, vmem, vmem, smem),
        scratch_shapes=[
            V((3, UNITS, 2048), BF),
            V((3, UNITS, 2048), BF),
            pltpu.SemaphoreType.DMA((3,)),
            pltpu.SemaphoreType.DMA((3,)),
        ],
        compiler_params=pltpu.CompilerParams(vmem_limit_bytes=60 << 20),
        name="scale",
    )(peaks, output, input_grad, wide, wdown)
    return (output, input_grad, gate_grad.T, up_grad.T, down_grad, amaxes)


def solution(mesh):
    placed = (
        P("hid", "tok"),
        P("tok", "hid"),
        P("tok", "hid"),
        P("hid", "tok"),
        P("hid", "tok"),
        P(),
    )
    return jax.shard_map(
        shards,
        mesh=mesh,
        in_specs=placed,
        out_specs=(
            P("hid", "tok"),
            P("hid", "tok"),
            P("tok", "hid"),
            P("tok", "hid"),
            P("hid", "tok"),
            P(),
        ),
        check_vma=False,
    )
```

```python
import jax
import jax.numpy as jnp
from jax import lax
from jax.experimental import pallas as pl
from jax.experimental.pallas import tpu as pltpu
from jax.sharding import PartitionSpec as P

MESH = pl.DeviceIdType.MESH
BF = jnp.bfloat16
F32 = jnp.float32
HALF = 1024
UNITS = 416
WIDE = 832


def contract_last(left, right):
    return lax.dot_general(left, right, (((1,), (1,)), ((), ())), preferred_element_type=F32)


def contract_first(left, right):
    return lax.dot_general(left, right, (((0,), (0,)), ((), ())), preferred_element_type=F32)


def quantize(value, scale):
    return jnp.clip(value / scale, -448.0, 448.0).astype(BF)


def fold(value):
    return jnp.concatenate([value[:, :512], value[:, 512:]], axis=0).astype(BF)


def unfold(value):
    value = value.astype(F32)
    return jnp.concatenate([value[:8], value[8:]], axis=1)


class Links:
    def __init__(self, send, recv):
        self.send, self.recv, self.used, self.open = send, recv, 0, []

    def slots(self, count):
        first = self.used
        self.used += count
        return first

    def copy(self, src, dst, slot, device):
        return pltpu.make_async_remote_copy(
            src_ref=src,
            dst_ref=dst,
            send_sem=self.send.at[slot],
            recv_sem=self.recv.at[slot],
            device_id=device,
            device_id_type=MESH,
        )

    def start(self, src, dst, slot, device):
        copy = self.copy(src, dst, slot, device)
        copy.start()
        self.open.append(copy)

    def arrived(self, dst, slot, device):
        self.copy(dst, dst, slot, device).wait_recv()

    def finish(self):
        for copy in self.open:
            copy.wait_send()


N_SEMS = 260


def kernel(
    prior, tokens, out_grad, gate_hbm, up_hbm, down_hbm,
    out_ref, in_grad_ref, wide_hbm, wdown_hbm, peaks_ref,
    xb, gb, wide_w, down_w, swap_out, swap_in,
    part, keep, got1, send2, got2,
    dpart, dkeep, dgot1, dsend2, dgot2,
    hb, db,
    o_refs, i_refs,
    wide_g, down_g, max_s, max_r,
    send_sem, recv_sem, load_sem, store_sem,
):
    t = lax.axis_index("tok")
    h = lax.axis_index("hid")
    y, zh, x, c = h // 16, (h // 8) % 2, (h // 2) % 4, h % 2
    p, s = t % 2, t // 2

    def device(dt=0, dy=0, dz=0, dx=0, dc=0):
        hid = ((((y + dy) % 4) * 2 + (zh + dz) % 2) * 4 + (x + dx) % 4) * 2 + (c + dc) % 2
        return ((t + dt) % 4, hid)

    def beside():
        return (t + 1 - 2 * p, h)

    peers = [device(dx=d, dc=e) for d in range(4) for e in range(2) if d or e]
    peers += [device(dy=d) for d in (1, 2, 3)]
    peers += [device(dt=d, dz=e) for d in range(4) for e in range(2) if d or e]
    peers += [device(dz=1, dc=1)]
    barrier = pltpu.get_barrier_semaphore()
    for peer in peers:
        pl.semaphore_signal(barrier, inc=1, device_id=peer, device_id_type=MESH)

    loads = [
        pltpu.make_async_copy(gate_hbm, wide_w.at[pl.ds(0, UNITS)], load_sem.at[0]),
        pltpu.make_async_copy(up_hbm, wide_w.at[pl.ds(UNITS, UNITS)], load_sem.at[1]),
        pltpu.make_async_copy(down_hbm, down_w, load_sem.at[2]),
    ]
    for load in loads:
        load.start()

    s0, s1, s2, s3 = [prior[i] / 448.0 for i in range(4)]
    mine = pl.ds(pl.multiple_of(c * HALF, HALF), HALF)
    other = pl.ds(pl.multiple_of((1 - c) * HALF, HALF), HALF)

    tok_f = tokens[...].astype(F32)
    og_f = out_grad[...].astype(F32)
    max_x = jnp.max(jnp.abs(tok_f))
    max_g = jnp.max(jnp.abs(og_f))
    for n, value in enumerate((quantize(tok_f, s0), quantize(og_f, s2))):
        value = value.astype(F32)
        swap_out[n, 0] = fold(value[:, :HALF])
        swap_out[n, 1] = fold(value[:, HALF:])

    links = Links(send_sem, recv_sem)
    core = device(dc=1)

    pl.semaphore_wait(barrier, len(peers))

    first = links.slots(5)
    away = device(dz=1)
    across = device(dz=1, dc=1)
    for n in (0, 1):
        links.start(swap_out.at[n, c], swap_in.at[1, n], first + 1 + 2 * n, away)
        links.start(swap_out.at[n, 1 - c], swap_in.at[2, n], first + 2 + 2 * n, across)
        if n == 0:
            links.start(swap_out.at[:, 1 - c], swap_in.at[0], first, core)

    def place(buf, z, own, theirs):
        own, theirs = unfold(own), unfold(theirs)
        low = jnp.where(c == 0, own, theirs)
        high = jnp.where(c == 0, theirs, own)
        buf[y, z, x, :, mine] = jnp.concatenate([low, high], axis=0).astype(BF)

    def place_far(n, buf):
        links.arrived(swap_in.at[1, n], first + 1 + 2 * n, away)
        links.arrived(swap_in.at[2, n], first + 2 + 2 * n, across)
        place(buf, 1 - zh, swap_in[1, n], swap_in[2, n])

    links.arrived(swap_in.at[0], first, core)
    place(xb, zh, swap_out[0, c], swap_in[0, 0])
    place(gb, zh, swap_out[1, c], swap_in[0, 1])
    def step_x(d):
        return device(dx=d)

    def step_y(d):
        return device(dy=d)

    cols_xy = pl.ds(pl.multiple_of(c * HALF, 512), 512)
    cols_yx = pl.ds(pl.multiple_of(c * HALF + 512, 512), 512)

    class Gather:
        def __init__(self, buf):
            self.buf = buf
            self.first = {a: (links.slots(4), links.slots(4)) for a in (0, 1)}
            self.second = {a: (links.slots(4), links.slots(4)) for a in (0, 1)}
            self.swap = {a: (links.slots(4), links.slots(4)) for a in (0, 1)}

        def level(self, a):
            return zh if a == 0 else 1 - zh

        def send_first(self, a):
            z = self.level(a)
            for d in (1, 3, 2):
                block = self.buf.at[y, z, x, :, cols_xy]
                links.start(block, block, self.first[a][0] + d, step_x(d))
                block = self.buf.at[y, z, x, :, cols_yx]
                links.start(block, block, self.first[a][1] + d, step_y(d))

        def wait_first(self, a):
            z = self.level(a)
            for d in (1, 3, 2):
                block = self.buf.at[y, z, (x - d) % 4, :, cols_xy]
                links.arrived(block, self.first[a][0] + d, step_x(4 - d))
                block = self.buf.at[(y - d) % 4, z, x, :, cols_yx]
                links.arrived(block, self.first[a][1] + d, step_y(4 - d))

        def send_second(self, a):
            z = self.level(a)
            for d in (1, 3, 2):
                rows = self.buf.at[y, z, :, :, cols_xy]
                links.start(rows, rows, self.second[a][0] + d, step_y(d))
                rows = self.buf.at[:, z, x, :, cols_yx]
                links.start(rows, rows, self.second[a][1] + d, step_x(d))

        def wait_second(self, a, d):
            z = self.level(a)
            rows = self.buf.at[(y - d) % 4, z, :, :, cols_xy]
            links.arrived(rows, self.second[a][0] + d, step_y(4 - d))
            rows = self.buf.at[:, z, (x - d) % 4, :, cols_yx]
            links.arrived(rows, self.second[a][1] + d, step_x(4 - d))

        def send_swap(self, a, d):
            z = self.level(a)
            rows = self.buf.at[(y - d) % 4, z, :, :, cols_xy]
            links.start(rows, rows, self.swap[a][0] + d, core)
            rows = self.buf.at[:, z, (x - d) % 4, :, cols_yx]
            links.start(rows, rows, self.swap[a][1] + d, core)

        def wait_swap(self, a):
            z = self.level(a)
            there_xy = pl.ds(pl.multiple_of((1 - c) * HALF, 512), 512)
            there_yx = pl.ds(pl.multiple_of((1 - c) * HALF + 512, 512), 512)
            for d in (0, 1, 3, 2):
                rows = self.buf.at[(y - d) % 4, z, :, :, there_xy]
                links.arrived(rows, self.swap[a][0] + d, core)
                rows = self.buf.at[:, z, (x - d) % 4, :, there_yx]
                links.arrived(rows, self.swap[a][1] + d, core)

        def complete(self, a):
            for d in (1, 3, 2):
                self.wait_second(a, d)
                self.send_swap(a, d)
            self.wait_swap(a)

    gx, gg = Gather(xb), Gather(gb)
    gx.send_first(0)
    gg.send_first(0)
    gx.wait_first(0)
    gx.send_second(0)
    place_far(0, xb)
    gx.send_first(1)
    place_far(1, gb)
    gg.send_first(1)
    gx.send_swap(0, 0)
    gg.wait_first(0)
    gg.send_second(0)
    gx.wait_first(1)
    gx.send_second(1)
    gg.wait_first(1)
    gg.send_second(1)
    gx.send_swap(1, 0)
    gg.send_swap(0, 0)
    gg.send_swap(1, 0)
    for load in loads:
        load.wait()
    gx.complete(0)

    order = ((1 - p) + 2 * (1 - s), (1 - p) + 2 * s, p + 2 * (1 - s), p + 2 * s)
    r1, r2 = links.slots(4), links.slots(2)
    d1, d2 = links.slots(2), links.slots(1)
    partner = beside()
    far = device(dt=2)
    units = (pl.ds(0, UNITS), pl.ds(UNITS, UNITS))
    lower = lax.broadcasted_iota(jnp.int32, (UNITS, 128), 1) < 64

    def turn(value):
        return pltpu.roll(value, 64, 1)

    def pair(buf, j, z=None):
        two = [buf[(y + k) % 4] if z is None else buf[(y + k) % 4, z] for k in order[j : j + 2]]
        return jnp.concatenate([value.reshape(-1, 2048) for value in two], axis=0)

    def gate_and_up(j, z):
        value = contract_last(wide_w[...], pair(xb, j, z))
        gate, up = value[:UNITS], value[UNITS:]
        return jnp.where(lower, gate, turn(up)), jnp.where(lower, turn(gate), up)

    for a, z in ((0, zh), (1, 1 - zh)):
        if a:
            gx.complete(1)
        for j, to, value in zip((0, 1), (1 - s, s), gate_and_up(0, z)):
            part[j, a] = value.astype(BF)
            links.start(part.at[j, a], got1.at[to, z], r1 + 2 * to + a, partner)
        for j, value in zip((0, 1), gate_and_up(2, z)):
            keep[j, z] = value

    def send_far(a, z):
        links.arrived(got1.at[1 - s, z], r1 + 2 * (1 - s) + a, partner)
        send2[z] = (keep[0, z] + got1[1 - s, z].astype(F32)).astype(BF)
        links.start(send2.at[z], got2.at[z], r2 + a, far)

    send_far(0, zh)
    gg.complete(0)
    gg.complete(1)
    value = contract_last(down_w[...], pair(gb, 0))
    dpart[0] = value[:, :128].astype(BF)
    dpart[1] = value[:, 128:].astype(BF)
    links.start(dpart.at[0], dgot1.at[1 - s], d1 + (1 - s), partner)
    value = contract_last(down_w[...], pair(gb, 2))
    dkeep[0] = value[:, :128]
    dkeep[1] = value[:, 128:]
    send_far(1, 1 - zh)
    links.arrived(dgot1.at[1 - s], d1 + (1 - s), partner)
    dsend2[...] = (dkeep[0] + dgot1[1 - s].astype(F32)).astype(BF)
    links.start(dsend2, dgot2, d2, far)
    links.start(dpart.at[1], dgot1.at[s], d1 + s, partner)
    yt = (y + t) % 4
    h1, h2, h3 = links.slots(1), links.slots(1), links.slots(1)
    g1, g2, g3 = links.slots(2), links.slots(2), links.slots(2)

    for a, z in ((0, zh), (1, 1 - zh)):
        links.arrived(got1.at[s, z], r1 + 2 * s + a, partner)
        links.arrived(got2.at[z], r2 + a, far)
    low, high = [
        (keep[1, z] + got1[s, z].astype(F32) + got2[z].astype(F32)) * s0 for z in (0, 1)
    ]
    gate = jnp.where(lower, low, turn(high))
    up = jnp.where(lower, turn(low), high)
    sig = jax.nn.sigmoid(gate)
    act = gate * sig
    hidden = act * up
    max_h = jnp.max(jnp.abs(hidden))
    hb[yt] = quantize(hidden, s1)
    links.start(hb.at[yt], hb.at[yt], h1, far)
    links.start(hb.at[yt], hb.at[yt], h2, partner)

    links.arrived(dgot1.at[s], d1 + s, partner)
    links.arrived(dgot2, d2, far)
    dhidden = (dkeep[1] + dgot1[s].astype(F32) + dgot2[...].astype(F32)) * s2
    dgate = dhidden * up * sig * (1.0 + gate * (1.0 - sig))
    dup = dhidden * act
    max_p = jnp.maximum(jnp.max(jnp.abs(dgate)), jnp.max(jnp.abs(dup)))
    for u, value in ((0, dgate), (1, dup)):
        db[yt, units[u]] = quantize(value, s3)
        links.start(db.at[yt, units[u]], db.at[yt, units[u]], g1 + u, far)
    for u in (0, 1):
        links.start(db.at[yt, units[u]], db.at[yt, units[u]], g2 + u, partner)
    yf = (y + (t + 2) % 4) % 4
    yp = (y + partner[0]) % 4
    ypf = (y + (partner[0] + 2) % 4) % 4
    links.arrived(hb.at[yf], h1, far)
    links.start(hb.at[yf], hb.at[yf], h3, partner)

    class Spread:
        def __init__(self, part, core_in, ring_y, ring_x, then_x, then_y, got_x, got_y, zs, fr, fold_out, fold_in):
            self.part, self.core_in, self.ring_y, self.ring_x = part, core_in, ring_y, ring_x
            self.then_x, self.then_y, self.got_x, self.got_y = then_x, then_y, got_x, got_y
            self.zs, self.fr, self.fold_out, self.fold_in = zs, fr, fold_out, fold_in
            self.cores, self.yx, self.xy = links.slots(4), links.slots(4), links.slots(16)
            self.x, self.y, self.z = links.slots(4), links.slots(4), links.slots(3)

        def block(self, n, left, right):
            value = contract_first(left, right)
            at = blocks[n]
            self.part[at] = value.astype(BF).reshape(2, 4, 16, 2048)
            links.start(self.part.at[at, :, :, :, other], self.core_in.at[at], self.cores + n, core)

        def first(self, n):
            at, d = blocks[n], steps[n]
            links.arrived(self.core_in.at[at], self.cores + n, core)
            value = self.part[at, :, :, :, mine].astype(F32) + self.core_in[at].astype(F32)
            self.core_in[at] = value.astype(BF)

            @pl.when(d != 0)
            def _():
                src = self.core_in.at[at, :, :, :, left]
                links.copy(src, self.ring_y.at[d - 1], self.yx + d, device(dy=d)).start()

            for e in (1, 3, 2):
                src = self.core_in.at[at, :, (x + e) % 4, :, right]
                links.start(src, self.ring_x.at[e - 1, at], self.xy + 4 * n + e, step_x(e))

        def second(self):
            for d in (1, 3, 2):
                links.arrived(self.ring_y.at[d - 1], self.yx + d, step_y(4 - d))
            total = self.core_in[y, :, :, :, left].astype(F32)
            for d in (1, 2, 3):
                total = total + self.ring_y[d - 1].astype(F32)
            self.then_x[...] = total.astype(BF)
            for d in (1, 3, 2):
                links.start(self.then_x.at[:, (x + d) % 4], self.got_x.at[d - 1], self.x + d, step_x(d))
            for n in range(4):
                for e in (1, 3, 2):
                    links.arrived(self.ring_x.at[e - 1, blocks[n]], self.xy + 4 * n + e, step_x(4 - e))
            total = self.core_in[:, :, x, :, right].astype(F32)
            for d in (1, 2, 3):
                total = total + self.ring_x[d - 1].astype(F32)
            self.then_y[...] = total.astype(BF)
            for d in (1, 3, 2):
                links.start(self.then_y.at[(y + d) % 4], self.got_y.at[d - 1], self.y + d, step_y(d))

        def third(self):
            for d in (1, 3, 2):
                links.arrived(self.got_x.at[d - 1], self.x + d, step_x(4 - d))
            total = self.then_x[:, x].astype(F32)
            for d in (1, 2, 3):
                total = total + self.got_x[d - 1].astype(F32)
            self.zs[:, :, left] = total
            for d in (1, 3, 2):
                links.arrived(self.got_y.at[d - 1], self.y + d, step_y(4 - d))
            total = self.then_y[y].astype(F32)
            for d in (1, 2, 3):
                total = total + self.got_y[d - 1].astype(F32)
            self.zs[:, :, right] = total
            self.fold_out[0] = fold(self.zs[1 - zh, rows_mine, :])
            self.fold_out[1] = fold(self.zs[1 - zh, rows_other, :])
            links.start(self.fold_out.at[0], self.fold_in.at[0], self.z + 1, away)
            links.start(self.fold_out.at[1], self.fold_in.at[1], self.z + 2, across)
            links.start(self.zs.at[zh, rows_other], self.fr, self.z, core)

        def last(self, ref, scale):
            links.arrived(self.fr, self.z, core)
            links.arrived(self.fold_in.at[0], self.z + 1, away)
            links.arrived(self.fold_in.at[1], self.z + 2, across)
            own = self.zs[zh, rows_mine, :] + unfold(self.fold_in[0])
            ref[:, mine] = (own * scale).astype(BF)
            ref[:, other] = ((self.fr[...] + unfold(self.fold_in[1])) * scale).astype(BF)

        def finish(self):
            for d in (1, 2, 3):
                src = self.core_in.at[0, :, :, :, left]
                links.copy(src, self.ring_y.at[0], self.yx + d, step_y(d)).wait_send()

    left, right = pl.ds(0, 512), pl.ds(512, 512)
    rows_other = pl.ds(pl.multiple_of((1 - c) * 8, 8), 8)
    rows_mine = pl.ds(pl.multiple_of(c * 8, 8), 8)
    steps = (t, (t + 2) % 4, partner[0], (partner[0] + 2) % 4)
    blocks = (yt, yf, yp, ypf)
    out_sum = Spread(*o_refs)
    in_sum = Spread(*i_refs)

    def pass_on():
        for u in (0, 1):
            links.arrived(db.at[yf, units[u]], g1 + u, far)
            links.start(db.at[yf, units[u]], db.at[yf, units[u]], g3 + u, partner)

    out_sum.block(0, hb[yt], down_w[...])
    out_sum.block(1, hb[yf], down_w[...])
    links.arrived(hb.at[yp], h2, partner)
    out_sum.block(2, hb[yp], down_w[...])
    in_sum.block(0, db[yt], wide_w[...])
    for n in range(3):
        out_sum.first(n)
    in_sum.first(0)
    pass_on()
    in_sum.block(1, db[yf], wide_w[...])
    links.arrived(hb.at[ypf], h3, partner)
    out_sum.block(3, hb[ypf], down_w[...])
    in_sum.first(1)

    hq_all = jnp.concatenate([hb[n] for n in range(4)], axis=1)

    def down_tile(i, top):
        columns = pl.ds(pl.multiple_of(i * 256, 256), 256)
        rows = gb[:, :, :, :, columns].reshape(512, 256)
        value = jnp.dot(hq_all, rows, preferred_element_type=F32)
        down_g[:, columns] = value.astype(BF)
        return jnp.maximum(top, jnp.max(jnp.abs(value)))

    max_d = lax.fori_loop(0, 4, down_tile, jnp.float32(0.0))
    out_sum.first(3)
    for u in (0, 1):
        links.arrived(db.at[yp, units[u]], g2 + u, partner)
    in_sum.block(2, db[yp], wide_w[...])
    max_d = lax.fori_loop(4, 8, down_tile, max_d)
    store_d = pltpu.make_async_copy(down_g, wdown_hbm, store_sem.at[0])
    store_d.start()
    in_sum.first(2)
    for u in (0, 1):
        links.arrived(db.at[ypf, units[u]], g3 + u, partner)
    in_sum.block(3, db[ypf], wide_w[...])

    dq_all = jnp.concatenate([db[n] for n in range(4)], axis=1)

    def wide_tile(i, top):
        columns = pl.ds(pl.multiple_of(i * 256, 256), 256)
        rows = xb[:, :, :, :, columns].reshape(512, 256)
        value = jnp.dot(dq_all, rows, preferred_element_type=F32)
        wide_g[:, columns] = value.astype(BF)
        return jnp.maximum(top, jnp.max(jnp.abs(value)))

    max_w = lax.fori_loop(0, 4, wide_tile, jnp.float32(0.0))
    in_sum.first(3)
    max_w = lax.fori_loop(4, 8, wide_tile, max_w)
    store_w = pltpu.make_async_copy(wide_g, wide_hbm, store_sem.at[1])
    store_w.start()

    row = lax.broadcasted_iota(jnp.int32, (8, 128), 0)
    by_wide, by_down = s0 * s3, s1 * s2
    marks = (max_x, max_h, max_g, max_p, max_w * by_wide, max_d * by_down, by_wide, by_down)
    tops = jnp.zeros((8, 128), F32)
    for n, value in enumerate(marks):
        tops = jnp.where(row == n, value, tops)

    def send_tops(stage, value, offsets):
        first = links.slots(len(offsets))
        max_s[stage] = value
        for n, offset in enumerate(offsets):
            links.start(max_s.at[stage], max_r.at[stage, n], first + n, device(**offset))
        return first

    def take_tops(stage, value, offsets, first):
        for n, offset in enumerate(offsets):
            back = {name: -d for name, d in offset.items()}
            links.arrived(max_r.at[stage, n], first + n, device(**back))
            value = jnp.maximum(value, max_r[stage, n])
        return value

    plane = [dict(dx=d, dc=e) for d in range(4) for e in range(2) if d or e]
    depth = [dict(dt=d, dz=e) for d in range(4) for e in range(2) if d or e]
    column = [dict(dy=d) for d in (1, 2, 3)]
    first = send_tops(0, tops, plane)
    out_sum.second()
    in_sum.second()
    tops = take_tops(0, tops, plane, first)
    first = send_tops(1, tops, column)
    out_sum.third()
    in_sum.third()
    tops = take_tops(1, tops, column, first)
    first = send_tops(2, tops, depth)
    out_sum.last(out_ref, s1)
    tops = take_tops(2, tops, depth, first)
    peaks_ref[pl.ds(0, 8), :] = tops
    peaks_ref[pl.ds(8, 8), :] = jnp.log(tops + 1e-6)
    in_sum.last(in_grad_ref, s3)

    out_sum.finish()
    in_sum.finish()
    links.finish()
    store_d.wait()
    store_w.wait()
    assert links.used <= N_SEMS


def scale_grads(
    peaks_hbm, out_in, in_grad_in, wide_hbm, wdown_hbm,
    gate_out, up_out, down_out, out_ref, in_grad_ref, amaxes_ref,
    held, scaled, peaks, load_sem, store_sem,
):
    sources = [wide_hbm.at[pl.ds(0, UNITS)], wide_hbm.at[pl.ds(UNITS, UNITS)], wdown_hbm]
    targets = [gate_out, up_out, down_out]
    loads = [
        pltpu.make_async_copy(source, held.at[n], load_sem.at[n]) for n, source in enumerate(sources)
    ]
    stores = [
        pltpu.make_async_copy(scaled.at[n], target, store_sem.at[n])
        for n, target in enumerate(targets)
    ]
    peaks_load = pltpu.make_async_copy(peaks_hbm, peaks, load_sem.at[3])
    peaks_load.start()
    for load in loads:
        load.start()
    passed = [
        pltpu.make_async_copy(out_in, out_ref, store_sem.at[3]),
        pltpu.make_async_copy(in_grad_in, in_grad_ref, store_sem.at[4]),
    ]
    for copy in passed:
        copy.start()
    peaks_load.wait()
    for n in range(6):
        amaxes_ref[n] = peaks[8 + n, 0]
    over_wide = peaks[6, 0] / (peaks[4, 0] + 1e-6)
    over_down = peaks[7, 0] / (peaks[5, 0] + 1e-6)
    for n in range(3):
        loads[n].wait()
        over = over_wide if n < 2 else over_down
        scaled[n] = (held[n].astype(F32) * over).astype(BF)
        stores[n].start()
    for store in stores + passed:
        store.wait()


def shards(tokens, gate_weight, up_weight, down_weight, out_grad, amax_prior):
    vmem = pl.BlockSpec(memory_space=pltpu.VMEM)
    hbm = pl.BlockSpec(memory_space=pl.ANY)
    V = pltpu.VMEM
    sum_scratch = (
        V((4, 2, 4, 16, 2048), BF), V((4, 2, 4, 16, HALF), BF),
        V((3, 2, 4, 16, 512), BF), V((3, 4, 2, 16, 512), BF),
        V((2, 4, 16, 512), BF), V((4, 2, 16, 512), BF),
        V((3, 2, 16, 512), BF), V((3, 2, 16, 512), BF),
        V((2, 16, HALF), F32), V((8, HALF), F32), V((2, 16, 512), BF), V((2, 16, 512), BF),
    )
    output, input_grad, wide, wdown, peaks = pl.pallas_call(
        kernel,
        out_shape=(
            jax.ShapeDtypeStruct((8, 2048), BF),
            jax.ShapeDtypeStruct((8, 2048), BF),
            jax.ShapeDtypeStruct((WIDE, 2048), BF),
            jax.ShapeDtypeStruct((UNITS, 2048), BF),
            jax.ShapeDtypeStruct((16, 128), F32),
        ),
        in_specs=[pl.BlockSpec(memory_space=pltpu.SMEM), vmem, vmem, hbm, hbm, hbm],
        out_specs=(vmem, vmem, hbm, hbm, vmem),
        scratch_shapes=[
            V((4, 2, 4, 16, 2048), BF), V((4, 2, 4, 16, 2048), BF),
            V((WIDE, 2048), BF), V((UNITS, 2048), BF),
            V((2, 2, 16, 512), BF), V((3, 2, 16, 512), BF),
            V((2, 2, UNITS, 128), BF), V((2, 2, UNITS, 128), F32), V((2, 2, UNITS, 128), BF),
            V((2, UNITS, 128), BF), V((2, UNITS, 128), BF),
            V((2, UNITS, 128), BF), V((2, UNITS, 128), F32), V((2, UNITS, 128), BF),
            V((UNITS, 128), BF), V((UNITS, 128), BF),
            V((4, UNITS, 128), BF), V((4, WIDE, 128), BF),
            sum_scratch, sum_scratch,
            V((WIDE, 2048), BF), V((UNITS, 2048), BF),
            V((3, 8, 128), F32), V((3, 7, 8, 128), F32),
            pltpu.SemaphoreType.DMA((N_SEMS,)), pltpu.SemaphoreType.DMA((N_SEMS,)),
            pltpu.SemaphoreType.DMA((3,)), pltpu.SemaphoreType.DMA((2,)),
        ],
        compiler_params=pltpu.CompilerParams(
            collective_id=0, has_side_effects=True, vmem_limit_bytes=60 << 20
        ),
        name="layer",
    )(amax_prior, tokens, out_grad, gate_weight.T, up_weight.T, down_weight)
    full = (
        jax.ShapeDtypeStruct((UNITS, 2048), BF),
        jax.ShapeDtypeStruct((UNITS, 2048), BF),
        jax.ShapeDtypeStruct((UNITS, 2048), BF),
        jax.ShapeDtypeStruct((8, 2048), BF),
        jax.ShapeDtypeStruct((8, 2048), BF),
        jax.ShapeDtypeStruct((6,), F32),
    )
    smem = pl.BlockSpec(memory_space=pltpu.SMEM)
    gate_grad, up_grad, down_grad, output, input_grad, amaxes = pl.pallas_call(
        scale_grads,
        out_shape=full,
        in_specs=[hbm] * 5,
        out_specs=(hbm, hbm, hbm, hbm, hbm, smem),
        scratch_shapes=[
            V((3, UNITS, 2048), BF),
            V((3, UNITS, 2048), BF),
            pltpu.SMEM((16, 128), F32),
            pltpu.SemaphoreType.DMA((4,)),
            pltpu.SemaphoreType.DMA((5,)),
        ],
        compiler_params=pltpu.CompilerParams(vmem_limit_bytes=60 << 20),
        name="scale",
    )(peaks, output, input_grad, wide, wdown)
    return (output, input_grad, gate_grad.T, up_grad.T, down_grad, amaxes)


def solution(mesh):
    placed = (
        P("hid", "tok"),
        P("tok", "hid"),
        P("tok", "hid"),
        P("hid", "tok"),
        P("hid", "tok"),
        P(),
    )
    return jax.shard_map(
        shards,
        mesh=mesh,
        in_specs=placed,
        out_specs=(
            P("hid", "tok"),
            P("hid", "tok"),
            P("tok", "hid"),
            P("tok", "hid"),
            P("hid", "tok"),
            P(),
        ),
        check_vma=False,
    )
```

```python
import jax
import jax.numpy as jnp
from jax import lax
from jax.experimental import pallas as pl
from jax.experimental.pallas import tpu as pltpu
from jax.sharding import PartitionSpec as P

MESH = pl.DeviceIdType.MESH
BF = jnp.bfloat16
F32 = jnp.float32
HALF = 1024
UNITS = 416
WIDE = 832


def contract_last(left, right):
    return lax.dot_general(left, right, (((1,), (1,)), ((), ())), preferred_element_type=F32)


def contract_first(left, right):
    return lax.dot_general(left, right, (((0,), (0,)), ((), ())), preferred_element_type=F32)


def quantize(value, scale):
    return jnp.clip(value / scale, -448.0, 448.0).astype(BF)


def fold(value):
    return jnp.concatenate([value[:, :512], value[:, 512:]], axis=0).astype(BF)


def unfold(value):
    value = value.astype(F32)
    return jnp.concatenate([value[:8], value[8:]], axis=1)


class Links:
    def __init__(self, send, recv):
        self.send, self.recv, self.used, self.open = send, recv, 0, []

    def slots(self, count):
        first = self.used
        self.used += count
        return first

    def copy(self, src, dst, slot, device):
        return pltpu.make_async_remote_copy(
            src_ref=src,
            dst_ref=dst,
            send_sem=self.send.at[slot],
            recv_sem=self.recv.at[slot],
            device_id=device,
            device_id_type=MESH,
        )

    def start(self, src, dst, slot, device):
        copy = self.copy(src, dst, slot, device)
        copy.start()
        self.open.append(copy)

    def arrived(self, dst, slot, device):
        self.copy(dst, dst, slot, device).wait_recv()

    def finish(self):
        for copy in self.open:
            copy.wait_send()


N_SEMS = 260


def kernel(
    prior, tokens, out_grad, gate_hbm, up_hbm, down_hbm,
    out_ref, in_grad_ref, wide_hbm, wdown_hbm, peaks_ref,
    xb, gb, wide_w, down_w, swap_out, swap_in,
    part, keep, got1, send2, got2,
    dpart, dkeep, dgot1, dsend2, dgot2,
    hb, db,
    o_refs, i_refs,
    wide_g, down_g, max_s, max_r,
    send_sem, recv_sem, load_sem, store_sem,
):
    t = lax.axis_index("tok")
    h = lax.axis_index("hid")
    y, zh, x, c = h // 16, (h // 8) % 2, (h // 2) % 4, h % 2
    p, s = t % 2, t // 2

    def device(dt=0, dy=0, dz=0, dx=0, dc=0):
        hid = ((((y + dy) % 4) * 2 + (zh + dz) % 2) * 4 + (x + dx) % 4) * 2 + (c + dc) % 2
        return ((t + dt) % 4, hid)

    def beside():
        return (t + 1 - 2 * p, h)

    peers = [device(dx=d, dc=e) for d in range(4) for e in range(2) if d or e]
    peers += [device(dy=d) for d in (1, 2, 3)]
    peers += [device(dt=d, dz=e) for d in range(4) for e in range(2) if d or e]
    peers += [device(dz=1, dc=1)]
    barrier = pltpu.get_barrier_semaphore()
    for peer in peers:
        pl.semaphore_signal(barrier, inc=1, device_id=peer, device_id_type=MESH)

    loads = [
        pltpu.make_async_copy(gate_hbm, wide_w.at[pl.ds(0, UNITS)], load_sem.at[0]),
        pltpu.make_async_copy(up_hbm, wide_w.at[pl.ds(UNITS, UNITS)], load_sem.at[1]),
        pltpu.make_async_copy(down_hbm, down_w, load_sem.at[2]),
    ]
    for load in loads:
        load.start()

    s0, s1, s2, s3 = [prior[i] / 448.0 for i in range(4)]
    mine = pl.ds(pl.multiple_of(c * HALF, HALF), HALF)
    other = pl.ds(pl.multiple_of((1 - c) * HALF, HALF), HALF)

    tok_f = tokens[...].astype(F32)
    og_f = out_grad[...].astype(F32)
    max_x = jnp.max(jnp.abs(tok_f))
    max_g = jnp.max(jnp.abs(og_f))
    for n, value in enumerate((quantize(tok_f, s0), quantize(og_f, s2))):
        value = value.astype(F32)
        swap_out[n, 0] = fold(value[:, :HALF])
        swap_out[n, 1] = fold(value[:, HALF:])

    links = Links(send_sem, recv_sem)
    core = device(dc=1)

    pl.semaphore_wait(barrier, len(peers))

    first = links.slots(5)
    away = device(dz=1)
    across = device(dz=1, dc=1)
    for n in (0, 1):
        links.start(swap_out.at[n, c], swap_in.at[1, n], first + 1 + 2 * n, away)
        links.start(swap_out.at[n, 1 - c], swap_in.at[2, n], first + 2 + 2 * n, across)
        if n == 0:
            links.start(swap_out.at[:, 1 - c], swap_in.at[0], first, core)

    def place(buf, z, own, theirs):
        own, theirs = unfold(own), unfold(theirs)
        low = jnp.where(c == 0, own, theirs)
        high = jnp.where(c == 0, theirs, own)
        buf[y, z, x, :, mine] = jnp.concatenate([low, high], axis=0).astype(BF)

    def place_far(n, buf):
        links.arrived(swap_in.at[1, n], first + 1 + 2 * n, away)
        links.arrived(swap_in.at[2, n], first + 2 + 2 * n, across)
        place(buf, 1 - zh, swap_in[1, n], swap_in[2, n])

    links.arrived(swap_in.at[0], first, core)
    place(xb, zh, swap_out[0, c], swap_in[0, 0])
    place(gb, zh, swap_out[1, c], swap_in[0, 1])
    def step_x(d):
        return device(dx=d)

    def step_y(d):
        return device(dy=d)

    cols_xy = pl.ds(pl.multiple_of(c * HALF, 512), 512)
    cols_yx = pl.ds(pl.multiple_of(c * HALF + 512, 512), 512)

    class Gather:
        def __init__(self, buf):
            self.buf = buf
            self.first = {a: (links.slots(4), links.slots(4)) for a in (0, 1)}
            self.second = {a: (links.slots(4), links.slots(4)) for a in (0, 1)}
            self.swap = {a: (links.slots(4), links.slots(4)) for a in (0, 1)}

        def level(self, a):
            return zh if a == 0 else 1 - zh

        def send_first(self, a):
            z = self.level(a)
            for d in (1, 3, 2):
                block = self.buf.at[y, z, x, :, cols_xy]
                links.start(block, block, self.first[a][0] + d, step_x(d))
                block = self.buf.at[y, z, x, :, cols_yx]
                links.start(block, block, self.first[a][1] + d, step_y(d))

        def wait_first(self, a):
            z = self.level(a)
            for d in (1, 3, 2):
                block = self.buf.at[y, z, (x - d) % 4, :, cols_xy]
                links.arrived(block, self.first[a][0] + d, step_x(4 - d))
                block = self.buf.at[(y - d) % 4, z, x, :, cols_yx]
                links.arrived(block, self.first[a][1] + d, step_y(4 - d))

        def send_second(self, a):
            z = self.level(a)
            for d in (1, 3, 2):
                rows = self.buf.at[y, z, :, :, cols_xy]
                links.start(rows, rows, self.second[a][0] + d, step_y(d))
                rows = self.buf.at[:, z, x, :, cols_yx]
                links.start(rows, rows, self.second[a][1] + d, step_x(d))

        def wait_second(self, a, d):
            z = self.level(a)
            rows = self.buf.at[(y - d) % 4, z, :, :, cols_xy]
            links.arrived(rows, self.second[a][0] + d, step_y(4 - d))
            rows = self.buf.at[:, z, (x - d) % 4, :, cols_yx]
            links.arrived(rows, self.second[a][1] + d, step_x(4 - d))

        def send_swap(self, a, d):
            z = self.level(a)
            rows = self.buf.at[(y - d) % 4, z, :, :, cols_xy]
            links.start(rows, rows, self.swap[a][0] + d, core)
            rows = self.buf.at[:, z, (x - d) % 4, :, cols_yx]
            links.start(rows, rows, self.swap[a][1] + d, core)

        def wait_swap(self, a):
            z = self.level(a)
            there_xy = pl.ds(pl.multiple_of((1 - c) * HALF, 512), 512)
            there_yx = pl.ds(pl.multiple_of((1 - c) * HALF + 512, 512), 512)
            for d in (0, 1, 3, 2):
                rows = self.buf.at[(y - d) % 4, z, :, :, there_xy]
                links.arrived(rows, self.swap[a][0] + d, core)
                rows = self.buf.at[:, z, (x - d) % 4, :, there_yx]
                links.arrived(rows, self.swap[a][1] + d, core)

        def complete(self, a):
            for d in (1, 3, 2):
                self.wait_second(a, d)
                self.send_swap(a, d)
            self.wait_swap(a)

    gx, gg = Gather(xb), Gather(gb)
    gx.send_first(0)
    gg.send_first(0)
    gx.wait_first(0)
    gx.send_second(0)
    place_far(0, xb)
    gx.send_first(1)
    place_far(1, gb)
    gg.send_first(1)
    gx.send_swap(0, 0)
    gg.wait_first(0)
    gg.send_second(0)
    gx.wait_first(1)
    gx.send_second(1)
    gg.wait_first(1)
    gg.send_second(1)
    gx.send_swap(1, 0)
    gg.send_swap(0, 0)
    gg.send_swap(1, 0)
    for load in loads:
        load.wait()
    gx.complete(0)

    order = ((1 - p) + 2 * (1 - s), (1 - p) + 2 * s, p + 2 * (1 - s), p + 2 * s)
    r1, r2 = links.slots(4), links.slots(2)
    d1, d2 = links.slots(2), links.slots(1)
    partner = beside()
    far = device(dt=2)
    units = (pl.ds(0, UNITS), pl.ds(UNITS, UNITS))
    lower = lax.broadcasted_iota(jnp.int32, (UNITS, 128), 1) < 64

    def turn(value):
        return pltpu.roll(value, 64, 1)

    def pair(buf, j, z=None):
        two = [buf[(y + k) % 4] if z is None else buf[(y + k) % 4, z] for k in order[j : j + 2]]
        return jnp.concatenate([value.reshape(-1, 2048) for value in two], axis=0)

    def gate_and_up(j, z):
        value = contract_last(wide_w[...], pair(xb, j, z))
        gate, up = value[:UNITS], value[UNITS:]
        return jnp.where(lower, gate, turn(up)), jnp.where(lower, turn(gate), up)

    for a, z in ((0, zh), (1, 1 - zh)):
        if a:
            gx.complete(1)
        for j, to, value in zip((0, 1), (1 - s, s), gate_and_up(0, z)):
            part[j, a] = value.astype(BF)
            links.start(part.at[j, a], got1.at[to, z], r1 + 2 * to + a, partner)
        for j, value in zip((0, 1), gate_and_up(2, z)):
            keep[j, z] = value

    def send_far(a, z):
        links.arrived(got1.at[1 - s, z], r1 + 2 * (1 - s) + a, partner)
        send2[z] = (keep[0, z] + got1[1 - s, z].astype(F32)).astype(BF)
        links.start(send2.at[z], got2.at[z], r2 + a, far)

    send_far(0, zh)
    gg.complete(0)
    gg.complete(1)
    value = contract_last(down_w[...], pair(gb, 0))
    dpart[0] = value[:, :128].astype(BF)
    dpart[1] = value[:, 128:].astype(BF)
    links.start(dpart.at[0], dgot1.at[1 - s], d1 + (1 - s), partner)
    value = contract_last(down_w[...], pair(gb, 2))
    dkeep[0] = value[:, :128]
    dkeep[1] = value[:, 128:]
    send_far(1, 1 - zh)
    links.arrived(dgot1.at[1 - s], d1 + (1 - s), partner)
    dsend2[...] = (dkeep[0] + dgot1[1 - s].astype(F32)).astype(BF)
    links.start(dsend2, dgot2, d2, far)
    links.start(dpart.at[1], dgot1.at[s], d1 + s, partner)
    yt = (y + t) % 4
    h1, h2, h3 = links.slots(1), links.slots(1), links.slots(1)
    g1, g2, g3 = links.slots(2), links.slots(2), links.slots(2)

    for a, z in ((0, zh), (1, 1 - zh)):
        links.arrived(got1.at[s, z], r1 + 2 * s + a, partner)
        links.arrived(got2.at[z], r2 + a, far)
    low, high = [
        (keep[1, z] + got1[s, z].astype(F32) + got2[z].astype(F32)) * s0 for z in (0, 1)
    ]
    gate = jnp.where(lower, low, turn(high))
    up = jnp.where(lower, turn(low), high)
    sig = jax.nn.sigmoid(gate)
    act = gate * sig
    hidden = act * up
    max_h = jnp.max(jnp.abs(hidden))
    hb[yt] = quantize(hidden, s1)
    links.start(hb.at[yt], hb.at[yt], h1, far)
    links.start(hb.at[yt], hb.at[yt], h2, partner)

    links.arrived(dgot1.at[s], d1 + s, partner)
    links.arrived(dgot2, d2, far)
    dhidden = (dkeep[1] + dgot1[s].astype(F32) + dgot2[...].astype(F32)) * s2
    dgate = dhidden * up * sig * (1.0 + gate * (1.0 - sig))
    dup = dhidden * act
    max_p = jnp.maximum(jnp.max(jnp.abs(dgate)), jnp.max(jnp.abs(dup)))
    for u, value in ((0, dgate), (1, dup)):
        db[yt, units[u]] = quantize(value, s3)
        links.start(db.at[yt, units[u]], db.at[yt, units[u]], g1 + u, far)
    for u in (0, 1):
        links.start(db.at[yt, units[u]], db.at[yt, units[u]], g2 + u, partner)
    yf = (y + (t + 2) % 4) % 4
    yp = (y + partner[0]) % 4
    ypf = (y + (partner[0] + 2) % 4) % 4
    links.arrived(hb.at[yf], h1, far)
    links.start(hb.at[yf], hb.at[yf], h3, partner)

    class Spread:
        def __init__(self, part, core_in, ring_y, ring_x, then_x, then_y, got_x, got_y, zs, fr, fold_out, fold_in):
            self.part, self.core_in, self.ring_y, self.ring_x = part, core_in, ring_y, ring_x
            self.then_x, self.then_y, self.got_x, self.got_y = then_x, then_y, got_x, got_y
            self.zs, self.fr, self.fold_out, self.fold_in = zs, fr, fold_out, fold_in
            self.cores, self.yx, self.xy = links.slots(4), links.slots(4), links.slots(16)
            self.x, self.y, self.z = links.slots(4), links.slots(4), links.slots(3)

        def block(self, n, left, right):
            value = contract_first(left, right)
            at = blocks[n]
            self.part[at] = value.astype(BF).reshape(2, 4, 16, 2048)
            links.start(self.part.at[at, :, :, :, other], self.core_in.at[at], self.cores + n, core)

        def first(self, n):
            at, d = blocks[n], steps[n]
            links.arrived(self.core_in.at[at], self.cores + n, core)
            value = self.part[at, :, :, :, mine].astype(F32) + self.core_in[at].astype(F32)
            self.core_in[at] = value.astype(BF)

            @pl.when(d != 0)
            def _():
                src = self.core_in.at[at, :, :, :, left]
                links.copy(src, self.ring_y.at[d - 1], self.yx + d, device(dy=d)).start()

            for e in (1, 3, 2):
                src = self.core_in.at[at, :, (x + e) % 4, :, right]
                links.start(src, self.ring_x.at[e - 1, at], self.xy + 4 * n + e, step_x(e))

        def second(self):
            for d in (1, 3, 2):
                links.arrived(self.ring_y.at[d - 1], self.yx + d, step_y(4 - d))
            total = self.core_in[y, :, :, :, left].astype(F32)
            for d in (1, 2, 3):
                total = total + self.ring_y[d - 1].astype(F32)
            self.then_x[...] = total.astype(BF)
            for d in (1, 3, 2):
                links.start(self.then_x.at[:, (x + d) % 4], self.got_x.at[d - 1], self.x + d, step_x(d))
            for n in range(4):
                for e in (1, 3, 2):
                    links.arrived(self.ring_x.at[e - 1, blocks[n]], self.xy + 4 * n + e, step_x(4 - e))
            total = self.core_in[:, :, x, :, right].astype(F32)
            for d in (1, 2, 3):
                total = total + self.ring_x[d - 1].astype(F32)
            self.then_y[...] = total.astype(BF)
            for d in (1, 3, 2):
                links.start(self.then_y.at[(y + d) % 4], self.got_y.at[d - 1], self.y + d, step_y(d))

        def third(self):
            for d in (1, 3, 2):
                links.arrived(self.got_x.at[d - 1], self.x + d, step_x(4 - d))
            total = self.then_x[:, x].astype(F32)
            for d in (1, 2, 3):
                total = total + self.got_x[d - 1].astype(F32)
            self.zs[:, :, left] = total
            for d in (1, 3, 2):
                links.arrived(self.got_y.at[d - 1], self.y + d, step_y(4 - d))
            total = self.then_y[y].astype(F32)
            for d in (1, 2, 3):
                total = total + self.got_y[d - 1].astype(F32)
            self.zs[:, :, right] = total
            self.fold_out[0] = fold(self.zs[1 - zh, rows_mine, :])
            self.fold_out[1] = fold(self.zs[1 - zh, rows_other, :])
            links.start(self.fold_out.at[0], self.fold_in.at[0], self.z + 1, away)
            links.start(self.fold_out.at[1], self.fold_in.at[1], self.z + 2, across)
            links.start(self.zs.at[zh, rows_other], self.fr, self.z, core)

        def last(self, ref, scale):
            links.arrived(self.fr, self.z, core)
            links.arrived(self.fold_in.at[0], self.z + 1, away)
            links.arrived(self.fold_in.at[1], self.z + 2, across)
            own = self.zs[zh, rows_mine, :] + unfold(self.fold_in[0])
            ref[:, mine] = (own * scale).astype(BF)
            ref[:, other] = ((self.fr[...] + unfold(self.fold_in[1])) * scale).astype(BF)

        def finish(self):
            for d in (1, 2, 3):
                src = self.core_in.at[0, :, :, :, left]
                links.copy(src, self.ring_y.at[0], self.yx + d, step_y(d)).wait_send()

    left, right = pl.ds(0, 512), pl.ds(512, 512)
    rows_other = pl.ds(pl.multiple_of((1 - c) * 8, 8), 8)
    rows_mine = pl.ds(pl.multiple_of(c * 8, 8), 8)
    steps = (t, (t + 2) % 4, partner[0], (partner[0] + 2) % 4)
    blocks = (yt, yf, yp, ypf)
    out_sum = Spread(*o_refs)
    in_sum = Spread(*i_refs)

    def pass_on():
        for u in (0, 1):
            links.arrived(db.at[yf, units[u]], g1 + u, far)
            links.start(db.at[yf, units[u]], db.at[yf, units[u]], g3 + u, partner)

    out_sum.block(0, hb[yt], down_w[...])
    out_sum.block(1, hb[yf], down_w[...])
    links.arrived(hb.at[yp], h2, partner)
    out_sum.block(2, hb[yp], down_w[...])
    in_sum.block(0, db[yt], wide_w[...])
    for n in range(3):
        out_sum.first(n)
    in_sum.first(0)
    pass_on()
    in_sum.block(1, db[yf], wide_w[...])
    links.arrived(hb.at[ypf], h3, partner)
    out_sum.block(3, hb[ypf], down_w[...])
    in_sum.first(1)

    hq_all = jnp.concatenate([hb[n] for n in range(4)], axis=1)

    def down_tile(i, top):
        columns = pl.ds(pl.multiple_of(i * 512, 512), 512)
        rows = gb[:, :, :, :, columns].reshape(512, 512)
        value = jnp.dot(hq_all, rows, preferred_element_type=F32)
        down_g[:, columns] = value.astype(BF)
        return jnp.maximum(top, jnp.max(jnp.abs(value)))

    max_d = lax.fori_loop(0, 2, down_tile, jnp.float32(0.0))
    out_sum.first(3)
    for u in (0, 1):
        links.arrived(db.at[yp, units[u]], g2 + u, partner)
    in_sum.block(2, db[yp], wide_w[...])
    max_d = lax.fori_loop(2, 4, down_tile, max_d)
    store_d = pltpu.make_async_copy(down_g, wdown_hbm, store_sem.at[0])
    store_d.start()
    in_sum.first(2)
    for u in (0, 1):
        links.arrived(db.at[ypf, units[u]], g3 + u, partner)
    in_sum.block(3, db[ypf], wide_w[...])

    dq_all = jnp.concatenate([db[n] for n in range(4)], axis=1)

    def wide_tile(i, top):
        columns = pl.ds(pl.multiple_of(i * 512, 512), 512)
        rows = xb[:, :, :, :, columns].reshape(512, 512)
        value = jnp.dot(dq_all, rows, preferred_element_type=F32)
        wide_g[:, columns] = value.astype(BF)
        return jnp.maximum(top, jnp.max(jnp.abs(value)))

    max_w = lax.fori_loop(0, 2, wide_tile, jnp.float32(0.0))
    in_sum.first(3)
    max_w = lax.fori_loop(2, 4, wide_tile, max_w)
    store_w = pltpu.make_async_copy(wide_g, wide_hbm, store_sem.at[1])
    store_w.start()

    row = lax.broadcasted_iota(jnp.int32, (8, 128), 0)
    by_wide, by_down = s0 * s3, s1 * s2
    marks = (max_x, max_h, max_g, max_p, max_w * by_wide, max_d * by_down, by_wide, by_down)
    tops = jnp.zeros((8, 128), F32)
    for n, value in enumerate(marks):
        tops = jnp.where(row == n, value, tops)

    def send_tops(stage, value, offsets):
        first = links.slots(len(offsets))
        max_s[stage] = value
        for n, offset in enumerate(offsets):
            links.start(max_s.at[stage], max_r.at[stage, n], first + n, device(**offset))
        return first

    def take_tops(stage, value, offsets, first):
        for n, offset in enumerate(offsets):
            back = {name: -d for name, d in offset.items()}
            links.arrived(max_r.at[stage, n], first + n, device(**back))
            value = jnp.maximum(value, max_r[stage, n])
        return value

    plane = [dict(dx=d, dc=e) for d in range(4) for e in range(2) if d or e]
    depth = [dict(dt=d, dz=e) for d in range(4) for e in range(2) if d or e]
    column = [dict(dy=d) for d in (1, 2, 3)]
    first = send_tops(0, tops, plane)
    out_sum.second()
    in_sum.second()
    tops = take_tops(0, tops, plane, first)
    first = send_tops(1, tops, column)
    out_sum.third()
    in_sum.third()
    tops = take_tops(1, tops, column, first)
    first = send_tops(2, tops, depth)
    out_sum.last(out_ref, s1)
    tops = take_tops(2, tops, depth, first)
    peaks_ref[pl.ds(0, 8), :] = tops
    peaks_ref[pl.ds(8, 8), :] = jnp.log(tops + 1e-6)
    in_sum.last(in_grad_ref, s3)

    out_sum.finish()
    in_sum.finish()
    links.finish()
    store_d.wait()
    store_w.wait()
    assert links.used <= N_SEMS


def scale_grads(
    peaks_hbm, out_in, in_grad_in, wide_hbm, wdown_hbm,
    gate_out, up_out, down_out, out_ref, in_grad_ref, amaxes_ref,
    held, scaled, peaks, load_sem, store_sem,
):
    sources = [wide_hbm.at[pl.ds(0, UNITS)], wide_hbm.at[pl.ds(UNITS, UNITS)], wdown_hbm]
    targets = [gate_out, up_out, down_out]
    loads = [
        pltpu.make_async_copy(source, held.at[n], load_sem.at[n]) for n, source in enumerate(sources)
    ]
    stores = [
        pltpu.make_async_copy(scaled.at[n], target, store_sem.at[n])
        for n, target in enumerate(targets)
    ]
    peaks_load = pltpu.make_async_copy(peaks_hbm, peaks, load_sem.at[3])
    peaks_load.start()
    for load in loads:
        load.start()
    passed = [
        pltpu.make_async_copy(out_in, out_ref, store_sem.at[3]),
        pltpu.make_async_copy(in_grad_in, in_grad_ref, store_sem.at[4]),
    ]
    for copy in passed:
        copy.start()
    peaks_load.wait()
    for n in range(6):
        amaxes_ref[n] = peaks[8 + n, 0]
    over_wide = peaks[6, 0] / (peaks[4, 0] + 1e-6)
    over_down = peaks[7, 0] / (peaks[5, 0] + 1e-6)
    for n in range(3):
        loads[n].wait()
        over = over_wide if n < 2 else over_down
        scaled[n] = (held[n].astype(F32) * over).astype(BF)
        stores[n].start()
    for store in stores + passed:
        store.wait()


def shards(tokens, gate_weight, up_weight, down_weight, out_grad, amax_prior):
    vmem = pl.BlockSpec(memory_space=pltpu.VMEM)
    hbm = pl.BlockSpec(memory_space=pl.ANY)
    V = pltpu.VMEM
    sum_scratch = (
        V((4, 2, 4, 16, 2048), BF), V((4, 2, 4, 16, HALF), BF),
        V((3, 2, 4, 16, 512), BF), V((3, 4, 2, 16, 512), BF),
        V((2, 4, 16, 512), BF), V((4, 2, 16, 512), BF),
        V((3, 2, 16, 512), BF), V((3, 2, 16, 512), BF),
        V((2, 16, HALF), F32), V((8, HALF), F32), V((2, 16, 512), BF), V((2, 16, 512), BF),
    )
    output, input_grad, wide, wdown, peaks = pl.pallas_call(
        kernel,
        out_shape=(
            jax.ShapeDtypeStruct((8, 2048), BF),
            jax.ShapeDtypeStruct((8, 2048), BF),
            jax.ShapeDtypeStruct((WIDE, 2048), BF),
            jax.ShapeDtypeStruct((UNITS, 2048), BF),
            jax.ShapeDtypeStruct((16, 128), F32),
        ),
        in_specs=[pl.BlockSpec(memory_space=pltpu.SMEM), vmem, vmem, hbm, hbm, hbm],
        out_specs=(vmem, vmem, hbm, hbm, vmem),
        scratch_shapes=[
            V((4, 2, 4, 16, 2048), BF), V((4, 2, 4, 16, 2048), BF),
            V((WIDE, 2048), BF), V((UNITS, 2048), BF),
            V((2, 2, 16, 512), BF), V((3, 2, 16, 512), BF),
            V((2, 2, UNITS, 128), BF), V((2, 2, UNITS, 128), F32), V((2, 2, UNITS, 128), BF),
            V((2, UNITS, 128), BF), V((2, UNITS, 128), BF),
            V((2, UNITS, 128), BF), V((2, UNITS, 128), F32), V((2, UNITS, 128), BF),
            V((UNITS, 128), BF), V((UNITS, 128), BF),
            V((4, UNITS, 128), BF), V((4, WIDE, 128), BF),
            sum_scratch, sum_scratch,
            V((WIDE, 2048), BF), V((UNITS, 2048), BF),
            V((3, 8, 128), F32), V((3, 7, 8, 128), F32),
            pltpu.SemaphoreType.DMA((N_SEMS,)), pltpu.SemaphoreType.DMA((N_SEMS,)),
            pltpu.SemaphoreType.DMA((3,)), pltpu.SemaphoreType.DMA((2,)),
        ],
        compiler_params=pltpu.CompilerParams(
            collective_id=0, has_side_effects=True, vmem_limit_bytes=60 << 20
        ),
        name="layer",
    )(amax_prior, tokens, out_grad, gate_weight.T, up_weight.T, down_weight)
    full = (
        jax.ShapeDtypeStruct((UNITS, 2048), BF),
        jax.ShapeDtypeStruct((UNITS, 2048), BF),
        jax.ShapeDtypeStruct((UNITS, 2048), BF),
        jax.ShapeDtypeStruct((8, 2048), BF),
        jax.ShapeDtypeStruct((8, 2048), BF),
        jax.ShapeDtypeStruct((6,), F32),
    )
    smem = pl.BlockSpec(memory_space=pltpu.SMEM)
    gate_grad, up_grad, down_grad, output, input_grad, amaxes = pl.pallas_call(
        scale_grads,
        out_shape=full,
        in_specs=[hbm] * 5,
        out_specs=(hbm, hbm, hbm, hbm, hbm, smem),
        scratch_shapes=[
            V((3, UNITS, 2048), BF),
            V((3, UNITS, 2048), BF),
            pltpu.SMEM((16, 128), F32),
            pltpu.SemaphoreType.DMA((4,)),
            pltpu.SemaphoreType.DMA((5,)),
        ],
        compiler_params=pltpu.CompilerParams(vmem_limit_bytes=60 << 20),
        name="scale",
    )(peaks, output, input_grad, wide, wdown)
    return (output, input_grad, gate_grad.T, up_grad.T, down_grad, amaxes)


def solution(mesh):
    placed = (
        P("hid", "tok"),
        P("tok", "hid"),
        P("tok", "hid"),
        P("hid", "tok"),
        P("hid", "tok"),
        P(),
    )
    return jax.shard_map(
        shards,
        mesh=mesh,
        in_specs=placed,
        out_specs=(
            P("hid", "tok"),
            P("hid", "tok"),
            P("tok", "hid"),
            P("tok", "hid"),
            P("hid", "tok"),
            P(),
        ),
        check_vma=False,
    )
```
